128 devices in a mesh: group: 2 (over core), blk: 64 (over z, y, x).
Axes of the slice: x: 4, y: 4, z: 4, core: 2. Of those that a mesh axis runs over, the one named last changes fastest.
Arguments:
- field: float32 [2, 64, 5, 32, 512], P('group', 'blk'), may hold values from -6 to 6
- source: float32 [2, 64, 5, 32, 512], P('group', 'blk'), may hold values from -6 to 6
- block_inverse: float32 [2, 64, 5, 5, 32, 512], P('group', 'blk'), may hold values from -0.05 to 0.14, as said below
- coupling: float32 [2, 64, 4, 32, 512], P('group', 'blk'), may hold values from 0.3 to 1.2
- donor_base: int32 [2, 64, 64, 256], P('group', 'blk'), may hold values from 0 to 15870
- donor_weight: float32 [2, 64, 4, 64, 256], P('group', 'blk'), may hold values from 0 to 1, as said below
- receiver_cell: int32 [2, 64, 64, 256], P('group', 'blk'), may hold values from 0 to 16384, as said below
Outputs:
- field_out: float32 [2, 64, 5, 32, 512], P('group', 'blk')
The draws below stay inside these ranges and needn't reach their ends.
Inputs may be any that keep to these rules, and one draw needn't show every extreme that they name: `block_inverse`: the entries of a block diagonal lie in 0.06 to 0.14; other entries are at most 0.05 in magnitude. `donor_weight`: the four weights of a slot are positive and sum to one. `receiver_cell`: within one block all entries below 16384 are distinct cells; for each donor block the used slots come first and the rest hold 16384; in every block some donor block fills all 256 slots.
All inputs are finite; a program needn't handle non-finite values.
Results may differ from the reference program's by a relative error of at most 0.0003.
Values sent between devices are 32-bit elements; how exact they have to be, the bound alone decides.
A program may use at most 128 MiB of HBM per device.

```python
import math
from functools import partial
import jax
import jax.numpy as jnp

NJ = 32
NK = 512
COMPONENTS = 5
SLOTS = 256
ITERS = 4
BLOCKS = 64
N_GROUP = 2


def draw_block_inverse(key, part):
    first, second = jax.random.split(jax.random.fold_in(key, 11))
    shape = (2, BLOCKS, COMPONENTS, COMPONENTS, NJ, NK)
    diag_shape = (2, BLOCKS, COMPONENTS, NJ, NK)
    diagonal = jnp.exp(jax.random.uniform(first, diag_shape, jnp.float32, math.log(0.06), math.log(0.14)))
    others = jnp.clip(0.015 * jax.random.normal(second, shape, jnp.float32), -0.05, 0.05)
    identity = jnp.eye(COMPONENTS, dtype=jnp.float32)[:, :, None, None]
    return others * (1.0 - identity) + identity * diagonal[:, :, :, None]


def draw_donor_weight(key, part):
    lower = 0.1
    raw = jax.random.uniform(jax.random.fold_in(key, 23), (2, BLOCKS, 4, BLOCKS, SLOTS), jnp.float32, lower, 1.0)
    return raw / jnp.sum(raw, axis=2, keepdims=True)


def receivers_of_block(key):
    first, second, third = jax.random.split(key, 3)
    cell_count = NJ * NK
    chosen = jax.random.permutation(first, cell_count)[:BLOCKS * SLOTS].reshape(BLOCKS, SLOTS).astype(jnp.int32)
    drawn = jax.random.randint(second, (BLOCKS,), 0, SLOTS + 1)
    counts = drawn * drawn // SLOTS
    fullest = jax.random.randint(third, (), 0, BLOCKS)
    counts = jnp.where(jnp.arange(BLOCKS) == fullest, SLOTS, counts)
    slot_iota = jnp.arange(SLOTS)
    return jnp.where(slot_iota[None, :] < counts[:, None], chosen, cell_count).astype(jnp.int32)


def draw_receiver_cell(key, part):
    keys = jax.random.split(jax.random.fold_in(key, 37), 2 * BLOCKS)
    return jax.vmap(receivers_of_block)(keys).reshape(2, BLOCKS, BLOCKS, SLOTS)


def set_ends(entries, rng, smallest, high):
    spot = [jax.random.randint(jax.random.fold_in(rng, axis), (), 0, length) for axis, length in enumerate(entries.shape)]
    main_axis = entries.shape.index(max(entries.shape))
    neighbour = spot[:main_axis] + [(spot[main_axis] + 1) % entries.shape[main_axis]] + spot[main_axis + 1:]
    return entries.at[tuple(spot)].set(smallest).at[tuple(neighbour)].set(high)


def shard_levels(key, extent, cuts, least, top_value):
    gain, own = 1.0, jax.random.fold_in(key, 6)
    for dim, parts in cuts:
        steps = jnp.exp(jax.random.uniform(jax.random.fold_in(own, dim), (parts,), jnp.float32, least / len(cuts), top_value / len(cuts)))
        gain = gain * jnp.repeat(steps, extent[dim] // parts).reshape([-1 if axis == dim else 1 for axis in range(len(extent))])
    return gain


def centred(stream_key, dims, scale, most, cuts=(), held_as=jnp.bfloat16):
    factor_of = shard_levels(stream_key, dims, cuts, -0.22, 0.18) if cuts else 1.0
    entries = jax.random.normal(stream_key, dims, jnp.float32) * scale * factor_of
    return jnp.minimum(jnp.maximum(entries, -most), most).astype(held_as)


def setup_inputs(seed: int = 0) -> dict:
    splits = jax.random.split(jax.random.key(seed), 8)
    field = centred(splits[0], (N_GROUP, BLOCKS, COMPONENTS, NJ, NK), 1.0, 6.0, ((0, 2), (1, 64)), jnp.float32)
    source = centred(splits[1], (N_GROUP, BLOCKS, COMPONENTS, NJ, NK), 1.0, 6.0, ((0, 2), (1, 64)), jnp.float32)
    block_inverse = draw_block_inverse(jax.random.fold_in(splits[7], 71), 0)
    coupling = jnp.clip(jnp.exp(math.log(1.2) - 1.3862944 * jax.random.uniform(splits[3], (N_GROUP, BLOCKS, 4, NJ, NK), jnp.float32) ** shard_levels(splits[3], (N_GROUP, BLOCKS, 4, NJ, NK), ((0, 2), (1, 64)), -0.2, 0.2)), 0.3, 1.2)
    donor_base = set_ends(jax.random.randint(splits[4], (N_GROUP, BLOCKS, BLOCKS, SLOTS), 0, (NJ - 1) * NK - 1), jax.random.fold_in(splits[4], 1), 0, ((NJ - 1) * NK - 1) - 1).astype(jnp.int32)
    donor_weight = draw_donor_weight(jax.random.fold_in(splits[7], 71), 0)
    receiver_cell = draw_receiver_cell(jax.random.fold_in(splits[7], 71), 0)
    return {"field": field, "source": source, "block_inverse": block_inverse, "coupling": coupling, "donor_base": donor_base, "donor_weight": donor_weight, "receiver_cell": receiver_cell}


upwind_offsets = (-3, -2, -1, 0, 1, 2)
upwind_weights = (-2.0 / 60.0, 15.0 / 60.0, -60.0 / 60.0, 20.0 / 60.0, 30.0 / 60.0, -3.0 / 60.0)


def window(padded, shift_j, shift_k, row_count, column_count):
    return padded[:, 3 + shift_j:3 + shift_j + row_count, 3 + shift_k:3 + shift_k + column_count]


def near_half(padded, solution, forcing, inverse, coupling, update_mask):
    row_count, column_count = solution.shape[1], solution.shape[2]
    gathered = coupling[0] * window(padded, -1, 0, row_count, column_count)
    gathered = gathered + coupling[1] * window(padded, 1, 0, row_count, column_count)
    gathered = gathered + coupling[2] * window(padded, 0, -1, row_count, column_count)
    gathered = gathered + coupling[3] * window(padded, 0, 1, row_count, column_count)
    total = forcing + gathered
    updated = jnp.sum(inverse * total[None], axis=1)
    return jnp.where(update_mask[None], updated, solution)


def off_section(padded, solution, forcing, inverse, coupling, update_mask):
    row_count, column_count = solution.shape[1], solution.shape[2]
    along_j = jnp.zeros_like(solution)
    along_k = jnp.zeros_like(solution)
    for offset, weight in zip(upwind_offsets, upwind_weights):
        along_j = along_j + weight * window(padded, offset, 0, row_count, column_count)
        along_k = along_k + weight * window(padded, 0, offset, row_count, column_count)
    residual_term = forcing - coupling[0] * along_j - coupling[1] * along_k
    updated = solution + jnp.sum(inverse * residual_term[None], axis=1)
    return jnp.where(update_mask[None], updated, solution)


def interpolate(flat_state, bases, weights, column_count):
    result = jnp.zeros((flat_state.shape[0],) + bases.shape, jnp.float32)
    for corner, offset in enumerate((0, 1, column_count, column_count + 1)):
        result = result + weights[corner][None] * flat_state[:, bases + offset]
    return result


def place(flat_state, targets, values):
    return flat_state.at[:, targets].set(values, mode="drop")


def mark(targets, cell_count):
    return jnp.zeros(cell_count, jnp.int32).at[targets].set(1, mode="drop")


def to_grid(array):
    moved = jnp.moveaxis(array, 0, -3)
    return moved.reshape(moved.shape[:-3] + (moved.shape[-3] * moved.shape[-2], moved.shape[-1]))


def from_grid(grid, block_count):
    pieces = grid.reshape(grid.shape[:-2] + (block_count, grid.shape[-2] // block_count, grid.shape[-1]))
    return jnp.moveaxis(pieces, -3, 0)


def pad_grid(grid):
    return jnp.pad(grid, ((0, 0), (3, 3), (3, 3)))


def reference(field, source, block_inverse, coupling, donor_base, donor_weight, receiver_cell):
    cell_count = NJ * NK
    targets = receiver_cell.reshape(2, BLOCKS, BLOCKS * SLOTS)
    frozen = jax.vmap(jax.vmap(partial(mark, cell_count=cell_count)))(targets).reshape(2, BLOCKS, NJ, NK)
    movable = [to_grid(frozen[0]) == 0, to_grid(frozen[1]) == 0]
    rows_iota = jax.lax.broadcasted_iota(jnp.int32, (BLOCKS * NJ, NK), 0)
    cols_iota = jax.lax.broadcasted_iota(jnp.int32, (BLOCKS * NJ, NK), 1)
    parity_grid = (rows_iota + cols_iota) % 2
    forcing = [to_grid(source[0]), to_grid(source[1])]
    inverse = [to_grid(block_inverse[0]), to_grid(block_inverse[1])]
    factors = [to_grid(coupling[0]), to_grid(coupling[1])]
    solution = field
    for iteration in range(ITERS):
        flat_state = solution.reshape(2, BLOCKS, COMPONENTS, cell_count)
        donor_values = jax.vmap(jax.vmap(partial(interpolate, column_count=NK)))(flat_state, donor_base, donor_weight)
        arrived = jnp.transpose(donor_values[::-1], (0, 3, 2, 1, 4)).reshape(2, BLOCKS, COMPONENTS, BLOCKS * SLOTS)
        flat_state = jax.vmap(jax.vmap(place))(flat_state, targets, arrived)
        solution = flat_state.reshape(2, BLOCKS, COMPONENTS, NJ, NK)
        near_grid = to_grid(solution[0])
        off_grid = to_grid(solution[1])
        for parity in range(2):
            near_grid = near_half(pad_grid(near_grid), near_grid, forcing[0], inverse[0], factors[0], movable[0] & (parity_grid == parity))
            off_grid = off_section(pad_grid(off_grid), off_grid, forcing[1], inverse[1], factors[1], movable[1])
        solution = jnp.stack([from_grid(near_grid, BLOCKS), from_grid(off_grid, BLOCKS)])
    return solution
```

```python
import functools

import jax
import jax.numpy as jnp
from jax import lax
from jax.experimental import pallas as pl
from jax.experimental.pallas import tpu as pltpu
from jax.sharding import PartitionSpec as P

ITERS = 4
V = 5
NJ = 32
NK = 512
S = 256
TOP = 8
G = 8

upwind_offsets = (-3, -2, -1, 0, 1, 2)
upwind_weights = (-2.0 / 60.0, 15.0 / 60.0, -60.0 / 60.0, 20.0 / 60.0, 30.0 / 60.0, -3.0 / 60.0)

f32, bf16, i32 = jnp.float32, jnp.bfloat16, jnp.int32
MESH = pl.DeviceIdType.MESH


def shift_k(x, o):
    if o == 0:
        return x
    n = x.shape[1]
    col = lax.broadcasted_iota(i32, x.shape, 1)
    rolled = pltpu.roll(x, (-o) % n, axis=1)
    keep = (col + o >= 0) & (col + o < n)
    return jnp.where(keep, rolled, 0.0)


def split(x):
    hi = x.astype(bf16)
    return hi, (x - hi.astype(f32)).astype(bf16)


def make_table(u, tab):
    zero = jnp.zeros((1, 1), f32)
    for v in range(V):
        a = u[0, v, TOP : TOP + NJ, :]
        first = jnp.concatenate([a[1:, :1], zero], axis=0)
        b = jnp.concatenate([a[:, 1:], first], axis=1)
        for i, t in enumerate((a, b)):
            hi, lo = split(t)
            tab[pl.ds(320 * i + 32 * v, 32), :] = hi
            tab[pl.ds(320 * i + 160 + 32 * v, 32), :] = lo


def interpolate(tab, base, w):
    k = base & (NK - 1)
    j = base >> 9
    hot = jnp.where(lax.broadcasted_iota(i32, (NK, S), 0) == k, 1.0, 0.0).astype(bf16)
    g = jnp.dot(tab[...], hot, preferred_element_type=f32)
    row = lax.broadcasted_iota(i32, (NJ, S), 0)
    here, below = row == j, row == j + 1
    p0 = jnp.where(here, w[0], jnp.where(below, w[2], 0.0))
    p1 = jnp.where(here, w[1], jnp.where(below, w[3], 0.0))
    rows = []
    for v in range(V):
        a = g[32 * v : 32 * v + 32] + g[160 + 32 * v : 192 + 32 * v]
        b = g[320 + 32 * v : 352 + 32 * v] + g[480 + 32 * v : 512 + 32 * v]
        rows.append(jnp.sum(a * p0 + b * p1, axis=0, keepdims=True))
    return jnp.concatenate(rows + [jnp.zeros((3, S), f32)], axis=0)


def kernel(
    blocks,
    field, source, inverse, coupling, base, weight, cell,
    out,
    u, tab, send, recv, acc, frozen, part, hsend, hrecv,
    send_sem, recv_sem, hsend_sem, hrecv_sem,
):
    g = lax.axis_index("group")
    b = lax.axis_index("blk")
    groups = blocks // G
    mine, within = b // G, b % G
    other = 1 - g
    is_near = g == 0
    has_low, has_high = b > 0, b < blocks - 1

    barrier = pltpu.get_barrier_semaphore()

    def greet(d, c):
        pl.semaphore_signal(barrier, inc=1, device_id=(other, d), device_id_type=MESH)
        return c

    lax.fori_loop(0, blocks, greet, 0)

    for d in ((b + blocks - 1) % blocks, (b + 1) % blocks):
        pl.semaphore_signal(barrier, inc=1, device_id=(g, d), device_id_type=MESH)

    for s in range(2):
        for v in range(V):
            u[s, v, 0:TOP, :] = jnp.zeros((TOP, NK), f32)
            u[s, v, TOP + NJ : TOP + NJ + 8, :] = jnp.zeros((8, NK), f32)
    for v in range(V):
        u[0, v, TOP : TOP + NJ, :] = field[v]
    hsend[...] = jnp.zeros_like(hsend)

    pl.semaphore_wait(barrier, blocks + 2)

    def message(it, i, d):
        return pltpu.make_async_remote_copy(
            src_ref=send.at[d],
            dst_ref=recv.at[it, b],
            send_sem=send_sem,
            recv_sem=recv_sem.at[it, i],
            device_id=(other, d),
            device_id_type=MESH,
        )

    def halo(n, side, target):
        return pltpu.make_async_remote_copy(
            src_ref=hsend.at[side],
            dst_ref=hrecv.at[n, 1 - side],
            send_sem=hsend_sem.at[side],
            recv_sem=hrecv_sem.at[n, 1 - side],
            device_id=(g, target),
            device_id_type=MESH,
        )

    for it in range(ITERS):
        make_table(u, tab)

        def gather_group(i, c):
            dg = (mine + i) % groups
            first = pl.multiple_of(dg * G, G)
            bases = base[pl.ds(first, G), :]
            ws = [weight[q, pl.ds(first, G), :] for q in range(4)]
            for q in range(G):
                send[first + q] = interpolate(
                    tab, bases[q : q + 1], [w[q : q + 1] for w in ws]
                )
            for q in range(G):
                message(it, i, first + (within + q) % G).start()
            return c

        lax.fori_loop(0, groups, gather_group, 0)

        acc[...] = jnp.zeros_like(acc)
        if it == 0:
            frozen[...] = jnp.zeros_like(frozen)

        def scatter_group(i, c):
            sg = (mine + groups - i) % groups
            first = pl.multiple_of(sg * G, G)
            pltpu.make_async_copy(
                recv.at[it, pl.ds(first, G)], recv.at[it, pl.ds(first, G)], recv_sem.at[it, i]
            ).wait()
            cells = cell[pl.ds(first, G), :]
            left, right = [], []
            for q in range(G):
                r = cells[q : q + 1]
                hit = lax.broadcasted_iota(i32, (NJ, S), 0) == (r >> 9)
                val = recv[it, first + q]
                hi = val.astype(bf16).astype(f32)
                rows = [
                    jnp.where(hit, t[v : v + 1], 0.0) for t in (hi, val - hi) for v in range(V)
                ]
                if it == 0:
                    rows.append(jnp.where(hit, 1.0, 0.0))
                left.append(jnp.concatenate(rows, axis=0).astype(bf16))
                right.append(
                    jnp.where(
                        lax.broadcasted_iota(i32, (NK, S), 0) == (r & (NK - 1)), 1.0, 0.0
                    ).astype(bf16)
                )
            p = lax.dot_general(
                jnp.concatenate(left, axis=1),
                jnp.concatenate(right, axis=1),
                (((1,), (1,)), ((), ())),
                preferred_element_type=f32,
            )
            acc[...] += p[:320]
            if it == 0:
                frozen[...] += p[320:]
            return c

        lax.fori_loop(0, groups, scatter_group, 0)

        pltpu.make_async_copy(send, send, send_sem).wait()

        fixed = frozen[...] > 0.5
        for v in range(V):
            placed = acc[32 * v : 32 * v + 32] + acc[160 + 32 * v : 192 + 32 * v]
            u[0, v, TOP : TOP + NJ, :] = jnp.where(fixed, placed, u[0, v, TOP : TOP + NJ, :])

        def half(h, c):
            n = 2 * it + h
            for v in range(V):
                hsend[0, 3 * v : 3 * v + 3, :] = u[h, v, TOP : TOP + 3, :]
                hsend[1, 3 * v : 3 * v + 3, :] = u[h, v, TOP + NJ - 3 : TOP + NJ, :]

            @pl.when(has_low)
            def _():
                halo(n, 0, b - 1).start()

            @pl.when(has_high)
            def _():
                halo(n, 1, b + 1).start()

            @pl.when(is_near)
            def _():
                for t in range(4):
                    rows = slice(8 * t, 8 * t + 8)
                    for v in range(V):
                        x = u[h, v, TOP + 8 * t : TOP + 8 * t + 8, :]
                        part[v, rows, :] = (
                            source[v, rows, :]
                            + coupling[2, rows, :] * shift_k(x, -1)
                            + coupling[3, rows, :] * shift_k(x, 1)
                        )

            @pl.when(jnp.logical_not(is_near))
            def _():
                for t in range(4):
                    rows = slice(8 * t, 8 * t + 8)
                    for v in range(V):
                        x = u[h, v, TOP + 8 * t : TOP + 8 * t + 8, :]
                        along = sum(a * shift_k(x, o) for o, a in zip(upwind_offsets, upwind_weights))
                        part[v, rows, :] = source[v, rows, :] - coupling[1, rows, :] * along

            @pl.when(has_low)
            def _():
                halo(n, 1, b - 1).wait_recv()
                for v in range(V):
                    u[h, v, TOP - 3 : TOP, :] = hrecv[n, 0, 3 * v : 3 * v + 3, :]

            @pl.when(has_high)
            def _():
                halo(n, 0, b + 1).wait_recv()
                for v in range(V):
                    u[h, v, TOP + NJ : TOP + NJ + 3, :] = hrecv[n, 1, 3 * v : 3 * v + 3, :]

            def apply(rows, ts, v):
                return sum(inverse[v, w, rows, :] * ts[w] for w in range(V))

            @pl.when(is_near)
            def _():
                for t in range(4):
                    rows = slice(8 * t, 8 * t + 8)
                    at = TOP + 8 * t
                    ts = [
                        part[v, rows, :]
                        + coupling[0, rows, :] * u[h, v, at - 1 : at + 7, :]
                        + coupling[1, rows, :] * u[h, v, at + 1 : at + 9, :]
                        for v in range(V)
                    ]
                    parity = (
                        lax.broadcasted_iota(i32, (8, NK), 0) + lax.broadcasted_iota(i32, (8, NK), 1) + h
                    ) % 2
                    update = (frozen[rows, :] < 0.5) & (parity == 0)
                    for v in range(V):
                        u[1 - h, v, at : at + 8, :] = jnp.where(
                            update, apply(rows, ts, v), u[h, v, at : at + 8, :]
                        )

            @pl.when(jnp.logical_not(is_near))
            def _():
                for t in range(4):
                    rows = slice(8 * t, 8 * t + 8)
                    at = TOP + 8 * t
                    ts = []
                    for v in range(V):
                        along = sum(
                            a * u[h, v, at + o : at + o + 8, :]
                            for o, a in zip(upwind_offsets, upwind_weights)
                        )
                        ts.append(part[v, rows, :] - coupling[0, rows, :] * along)
                    update = frozen[rows, :] < 0.5
                    for v in range(V):
                        old = u[h, v, at : at + 8, :]
                        u[1 - h, v, at : at + 8, :] = jnp.where(update, old + apply(rows, ts, v), old)

            @pl.when(has_low)
            def _():
                halo(n, 0, b - 1).wait_send()

            @pl.when(has_high)
            def _():
                halo(n, 1, b + 1).wait_send()

            return c

        lax.fori_loop(0, 2, half, 0)

    for v in range(V):
        out[v] = u[0, v, TOP : TOP + NJ, :]


def on_device(field, source, block_inverse, coupling, donor_base, donor_weight, receiver_cell):
    blocks = donor_base.shape[2]
    vmem = pl.BlockSpec(memory_space=pltpu.VMEM)
    result = pl.pallas_call(
        functools.partial(kernel, blocks),
        out_shape=jax.ShapeDtypeStruct((V, NJ, NK), f32),
        in_specs=[vmem] * 7,
        out_specs=vmem,
        scratch_shapes=[
            pltpu.VMEM((2, V, TOP + NJ + 8, NK), f32),
            pltpu.VMEM((640, NK), bf16),
            pltpu.VMEM((blocks, 8, S), f32),
            pltpu.VMEM((ITERS, blocks, 8, S), f32),
            pltpu.VMEM((320, NK), f32),
            pltpu.VMEM((NJ, NK), f32),
            pltpu.VMEM((V, NJ, NK), f32),
            pltpu.VMEM((2, 16, NK), f32),
            pltpu.VMEM((2 * ITERS, 2, 16, NK), f32),
            pltpu.SemaphoreType.DMA,
            pltpu.SemaphoreType.DMA((ITERS, blocks // G)),
            pltpu.SemaphoreType.DMA((2,)),
            pltpu.SemaphoreType.DMA((2 * ITERS, 2)),
        ],
        compiler_params=pltpu.CompilerParams(
            collective_id=0, has_side_effects=True, vmem_limit_bytes=48 * 2**20
        ),
    )(
        field[0, 0],
        source[0, 0],
        block_inverse[0, 0],
        coupling[0, 0],
        donor_base[0, 0],
        donor_weight[0, 0],
        receiver_cell[0, 0],
    )
    return result[None, None]


def solution(mesh):
    in_specs = (
        P("group", "blk", None, None, None),
        P("group", "blk", None, None, None),
        P("group", "blk", None, None, None, None),
        P("group", "blk", None, None, None),
        P("group", "blk", None, None),
        P("group", "blk", None, None, None),
        P("group", "blk", None, None),
    )
    out_specs = P("group", "blk", None, None, None)
    return jax.shard_map(
        on_device, mesh=mesh, in_specs=in_specs, out_specs=out_specs, check_vma=False
    )
```

```python
import functools

import jax
import jax.numpy as jnp
from jax import lax
from jax.experimental import pallas as pl
from jax.experimental.pallas import tpu as pltpu
from jax.sharding import PartitionSpec as P

ITERS = 4
V = 5
NJ = 32
NK = 512
S = 256
TOP = 8
G = 8

upwind_offsets = (-3, -2, -1, 0, 1, 2)
upwind_weights = (-2.0 / 60.0, 15.0 / 60.0, -60.0 / 60.0, 20.0 / 60.0, 30.0 / 60.0, -3.0 / 60.0)

f32, bf16, i32 = jnp.float32, jnp.bfloat16, jnp.int32
MESH = pl.DeviceIdType.MESH


def shift_k(x, o):
    if o == 0:
        return x
    n = x.shape[1]
    col = lax.broadcasted_iota(i32, x.shape, 1)
    rolled = pltpu.roll(x, (-o) % n, axis=1)
    keep = (col + o >= 0) & (col + o < n)
    return jnp.where(keep, rolled, 0.0)


def split(x):
    hi = x.astype(bf16)
    return hi, (x - hi.astype(f32)).astype(bf16)


def make_table(u, tab):
    for v in range(V):
        hl = jnp.concatenate(split(u[0, v, TOP : TOP + NJ, :]), axis=0)
        for e in range(2):
            pick = jnp.where(
                lax.broadcasted_iota(i32, (NK, NK // 2), 0)
                == 2 * lax.broadcasted_iota(i32, (NK, NK // 2), 1) + e,
                1.0,
                0.0,
            ).astype(bf16)
            t = jnp.dot(hl, pick, preferred_element_type=f32)
            parts = [(e, t)]
            if e == 0:
                first = jnp.concatenate([t[1:, :1], jnp.zeros((1, 1), f32)], axis=0)
                parts.append((2, jnp.concatenate([t[:, 1:], first], axis=1)))
            for o, p in parts:
                p = p.astype(bf16)
                tab[pl.ds(160 * o + 32 * v, 32), :] = p[:32]
                tab[pl.ds(480 + 160 * o + 32 * v, 32), :] = p[32:]


def one_hot(base):
    k = (base & (NK - 1)) >> 1
    return jnp.where(lax.broadcasted_iota(i32, (NK // 2, S), 0) == k, 1.0, 0.0).astype(bf16)


def patterns(base, w):
    even = (base & 1) == 0
    row = lax.broadcasted_iota(i32, (NJ, S), 0)
    here, below = row == (base >> 9), row == (base >> 9) + 1
    zero = jnp.zeros_like(w[0])

    def spread(x, y):
        return jnp.where(here, x, jnp.where(below, y, 0.0))

    return (
        spread(jnp.where(even, w[0], zero), jnp.where(even, w[2], zero)),
        spread(jnp.where(even, w[1], w[0]), jnp.where(even, w[3], w[2])),
        spread(jnp.where(even, zero, w[1]), jnp.where(even, zero, w[3])),
    )


def interpolate(tab, hot, ps):
    g = jnp.dot(tab[...], hot, preferred_element_type=f32)
    rows = []
    for v in range(V):
        total = None
        for o in range(3):
            at = 160 * o + 32 * v
            term = (g[at : at + 32] + g[480 + at : 512 + at]) * ps[o]
            total = term if total is None else total + term
        rows.append(jnp.sum(total, axis=0, keepdims=True))
    return jnp.concatenate(rows + [jnp.zeros((3, S), f32)], axis=0)


def kernel(
    blocks,
    field_hbm, source_hbm, inverse_hbm, coupling_hbm, base_hbm, weight_hbm, cell_hbm,
    out,
    source, inverse, coupling, base, weight, cell,
    u, tab, hots, pats, send, recv, acc, frozen, part, hsend, hrecv,
    send_sem, recv_sem, hsend_sem, hrecv_sem, in_sem,
):
    g = lax.axis_index("group")
    b = lax.axis_index("blk")
    groups = blocks // G
    mine, within = b // G, b % G
    other = 1 - g
    is_near = g == 0
    has_low, has_high = b > 0, b < blocks - 1

    def block_rows(ref):
        return ref.at[0, :, pl.ds(TOP, NJ), :]

    loads = [
        pltpu.make_async_copy(a, c, in_sem.at[n])
        for n, (a, c) in enumerate(
            (
                (field_hbm, block_rows(u)),
                (base_hbm, base),
                (weight_hbm, weight),
                (cell_hbm, cell),
                (source_hbm, source),
                (coupling_hbm, coupling),
                (inverse_hbm, inverse),
            )
        )
    ]
    for load in loads:
        load.start()

    barrier = pltpu.get_barrier_semaphore()

    def greet(d, c):
        pl.semaphore_signal(barrier, inc=1, device_id=(other, d), device_id_type=MESH)
        return c

    lax.fori_loop(0, blocks, greet, 0)

    for d in ((b + blocks - 1) % blocks, (b + 1) % blocks):
        pl.semaphore_signal(barrier, inc=1, device_id=(g, d), device_id_type=MESH)

    for s in range(2):
        for v in range(V):
            u[s, v, 0:TOP, :] = jnp.zeros((TOP, NK), f32)
            u[s, v, TOP + NJ : TOP + NJ + 8, :] = jnp.zeros((8, NK), f32)
    hsend[...] = jnp.zeros_like(hsend)

    for load in loads[:3]:
        load.wait()

    def message(it, i, d):
        return pltpu.make_async_remote_copy(
            src_ref=send.at[d],
            dst_ref=recv.at[it, b],
            send_sem=send_sem,
            recv_sem=recv_sem.at[it, i],
            device_id=(other, d),
            device_id_type=MESH,
        )

    def halo(n, side, target):
        return pltpu.make_async_remote_copy(
            src_ref=hsend.at[side],
            dst_ref=hrecv.at[n, 1 - side],
            send_sem=hsend_sem.at[side],
            recv_sem=hrecv_sem.at[n, 1 - side],
            device_id=(g, target),
            device_id_type=MESH,
        )

    for it in range(ITERS):
        make_table(u, tab)

        def gather_group(i, c):
            dg = (mine + i) % groups
            first = pl.multiple_of(dg * G, G)
            if it == 0:
                bases = base[pl.ds(first, G), :]
                ws = [weight[q, pl.ds(first, G), :] for q in range(4)]
            for q in range(G):
                if it == 0:
                    hot = one_hot(bases[q : q + 1])
                    ps = patterns(bases[q : q + 1], [w[q : q + 1] for w in ws])
                    hots[first + q] = hot
                    for o in range(3):
                        pats[first + q, o] = ps[o]
                else:
                    hot = hots[first + q]
                    ps = [pats[first + q, o] for o in range(3)]
                send[first + q] = interpolate(tab, hot, ps)
            if it == 0:

                @pl.when(i == 0)
                def _():
                    pl.semaphore_wait(barrier, blocks + 2)

            for q in range(G):
                message(it, i, first + (within + q) % G).start()
            return c

        lax.fori_loop(0, groups, gather_group, 0)

        acc[...] = jnp.zeros_like(acc)
        if it == 0:
            frozen[...] = jnp.zeros_like(frozen)
            loads[3].wait()

        def scatter_group(i, c):
            sg = (mine + groups - i) % groups
            first = pl.multiple_of(sg * G, G)
            pltpu.make_async_copy(
                recv.at[it, pl.ds(first, G)], recv.at[it, pl.ds(first, G)], recv_sem.at[it, i]
            ).wait()
            cells = cell[pl.ds(first, G), :]
            left, right = [], []
            for q in range(G):
                r = cells[q : q + 1]
                hit = lax.broadcasted_iota(i32, (NJ, S), 0) == (r >> 9)
                val = recv[it, first + q]
                hi = val.astype(bf16).astype(f32)
                rows = [
                    jnp.where(hit, t[v : v + 1], 0.0) for t in (hi, val - hi) for v in range(V)
                ]
                if it == 0:
                    rows.append(jnp.where(hit, 1.0, 0.0))
                left.append(jnp.concatenate(rows, axis=0).astype(bf16))
                right.append(
                    jnp.where(
                        lax.broadcasted_iota(i32, (NK, S), 0) == (r & (NK - 1)), 1.0, 0.0
                    ).astype(bf16)
                )
            p = lax.dot_general(
                jnp.concatenate(left, axis=1),
                jnp.concatenate(right, axis=1),
                (((1,), (1,)), ((), ())),
                preferred_element_type=f32,
            )
            acc[...] += p[:320]
            if it == 0:
                frozen[...] += p[320:]
            return c

        lax.fori_loop(0, groups, scatter_group, 0)

        pltpu.make_async_copy(send, send, send_sem).wait()

        fixed = frozen[...] > 0.5
        for v in range(V):
            placed = acc[32 * v : 32 * v + 32] + acc[160 + 32 * v : 192 + 32 * v]
            u[0, v, TOP : TOP + NJ, :] = jnp.where(fixed, placed, u[0, v, TOP : TOP + NJ, :])

        if it == 0:
            for load in loads[4:]:
                load.wait()

        def half(h, c):
            n = 2 * it + h
            for v in range(V):
                hsend[0, 3 * v : 3 * v + 3, :] = u[h, v, TOP : TOP + 3, :]
                hsend[1, 3 * v : 3 * v + 3, :] = u[h, v, TOP + NJ - 3 : TOP + NJ, :]

            @pl.when(has_low)
            def _():
                halo(n, 0, b - 1).start()

            @pl.when(has_high)
            def _():
                halo(n, 1, b + 1).start()

            def apply(rows, ts, v):
                return sum(inverse[v, w, rows, :] * ts[w] for w in range(V))

            def near_k(v, rows, at):
                x = u[h, v, at : at + 8, :]
                return (
                    source[v, rows, :]
                    + coupling[2, rows, :] * shift_k(x, -1)
                    + coupling[3, rows, :] * shift_k(x, 1)
                )

            def near_rest(rows, at, along_k):
                ts = [
                    along_k[v]
                    + coupling[0, rows, :] * u[h, v, at - 1 : at + 7, :]
                    + coupling[1, rows, :] * u[h, v, at + 1 : at + 9, :]
                    for v in range(V)
                ]
                parity = (
                    lax.broadcasted_iota(i32, (8, NK), 0) + lax.broadcasted_iota(i32, (8, NK), 1) + h
                ) % 2
                update = (frozen[rows, :] < 0.5) & (parity == 0)
                for v in range(V):
                    u[1 - h, v, at : at + 8, :] = jnp.where(
                        update, apply(rows, ts, v), u[h, v, at : at + 8, :]
                    )

            def off_k(v, rows, at):
                x = u[h, v, at : at + 8, :]
                along = sum(a * shift_k(x, o) for o, a in zip(upwind_offsets, upwind_weights))
                return source[v, rows, :] - coupling[1, rows, :] * along

            def off_rest(rows, at, along_k):
                ts = []
                for v in range(V):
                    along = sum(
                        a * u[h, v, at + o : at + o + 8, :]
                        for o, a in zip(upwind_offsets, upwind_weights)
                    )
                    ts.append(along_k[v] - coupling[0, rows, :] * along)
                update = frozen[rows, :] < 0.5
                for v in range(V):
                    old = u[h, v, at : at + 8, :]
                    u[1 - h, v, at : at + 8, :] = jnp.where(update, old + apply(rows, ts, v), old)

            def before(of_k, rest):
                for t in range(4):
                    rows, at = slice(8 * t, 8 * t + 8), TOP + 8 * t
                    along_k = [of_k(v, rows, at) for v in range(V)]
                    if t in (1, 2):
                        rest(rows, at, along_k)
                    else:
                        for v in range(V):
                            part[v, rows, :] = along_k[v]

            def after(rest):
                for t in (0, 3):
                    rows, at = slice(8 * t, 8 * t + 8), TOP + 8 * t
                    rest(rows, at, [part[v, rows, :] for v in range(V)])

            @pl.when(is_near)
            def _():
                before(near_k, near_rest)

            @pl.when(jnp.logical_not(is_near))
            def _():
                before(off_k, off_rest)

            @pl.when(has_low)
            def _():
                halo(n, 1, b - 1).wait_recv()
                for v in range(V):
                    u[h, v, TOP - 3 : TOP, :] = hrecv[n, 0, 3 * v : 3 * v + 3, :]

            @pl.when(has_high)
            def _():
                halo(n, 0, b + 1).wait_recv()
                for v in range(V):
                    u[h, v, TOP + NJ : TOP + NJ + 3, :] = hrecv[n, 1, 3 * v : 3 * v + 3, :]

            @pl.when(is_near)
            def _():
                after(near_rest)

            @pl.when(jnp.logical_not(is_near))
            def _():
                after(off_rest)

            @pl.when(has_low)
            def _():
                halo(n, 0, b - 1).wait_send()

            @pl.when(has_high)
            def _():
                halo(n, 1, b + 1).wait_send()

            return c

        lax.fori_loop(0, 2, half, 0)

    store = pltpu.make_async_copy(block_rows(u), out, in_sem.at[0])
    store.start()
    store.wait()


def on_device(field, source, block_inverse, coupling, donor_base, donor_weight, receiver_cell):
    blocks = donor_base.shape[2]
    hbm = pl.BlockSpec(memory_space=pl.ANY)
    result = pl.pallas_call(
        functools.partial(kernel, blocks),
        out_shape=jax.ShapeDtypeStruct((V, NJ, NK), f32),
        in_specs=[hbm] * 7,
        out_specs=hbm,
        scratch_shapes=[
            pltpu.VMEM((V, NJ, NK), f32),
            pltpu.VMEM((V, V, NJ, NK), f32),
            pltpu.VMEM((4, NJ, NK), f32),
            pltpu.VMEM((blocks, S), i32),
            pltpu.VMEM((4, blocks, S), f32),
            pltpu.VMEM((blocks, S), i32),
            pltpu.VMEM((2, V, TOP + NJ + 8, NK), f32),
            pltpu.VMEM((960, NK // 2), bf16),
            pltpu.VMEM((blocks, NK // 2, S), bf16),
            pltpu.VMEM((blocks, 3, NJ, S), f32),
            pltpu.VMEM((blocks, 8, S), f32),
            pltpu.VMEM((ITERS, blocks, 8, S), f32),
            pltpu.VMEM((320, NK), f32),
            pltpu.VMEM((NJ, NK), f32),
            pltpu.VMEM((V, NJ, NK), f32),
            pltpu.VMEM((2, 16, NK), f32),
            pltpu.VMEM((2 * ITERS, 2, 16, NK), f32),
            pltpu.SemaphoreType.DMA,
            pltpu.SemaphoreType.DMA((ITERS, blocks // G)),
            pltpu.SemaphoreType.DMA((2,)),
            pltpu.SemaphoreType.DMA((2 * ITERS, 2)),
            pltpu.SemaphoreType.DMA((7,)),
        ],
        compiler_params=pltpu.CompilerParams(
            collective_id=0, has_side_effects=True, vmem_limit_bytes=48 * 2**20
        ),
    )(
        field[0, 0],
        source[0, 0],
        block_inverse[0, 0],
        coupling[0, 0],
        donor_base[0, 0],
        donor_weight[0, 0],
        receiver_cell[0, 0],
    )
    return result[None, None]


def solution(mesh):
    in_specs = (
        P("group", "blk", None, None, None),
        P("group", "blk", None, None, None),
        P("group", "blk", None, None, None, None),
        P("group", "blk", None, None, None),
        P("group", "blk", None, None),
        P("group", "blk", None, None, None),
        P("group", "blk", None, None),
    )
    out_specs = P("group", "blk", None, None, None)
    return jax.shard_map(
        on_device, mesh=mesh, in_specs=in_specs, out_specs=out_specs, check_vma=False
    )
```

```python
import functools

import jax
import jax.numpy as jnp
from jax import lax
from jax.experimental import pallas as pl
from jax.experimental.pallas import tpu as pltpu
from jax.sharding import PartitionSpec as P

ITERS = 4
V = 5
NJ = 32
NK = 512
S = 256
TOP = 16
G = 8

upwind_offsets = (-3, -2, -1, 0, 1, 2)
upwind_weights = (-2.0 / 60.0, 15.0 / 60.0, -60.0 / 60.0, 20.0 / 60.0, 30.0 / 60.0, -3.0 / 60.0)

f32, bf16, i32 = jnp.float32, jnp.bfloat16, jnp.int32
MESH = pl.DeviceIdType.MESH


def shift_k(x, o):
    if o == 0:
        return x
    n = x.shape[1]
    col = lax.broadcasted_iota(i32, x.shape, 1)
    rolled = pltpu.roll(x, (-o) % n, axis=1)
    keep = (col + o >= 0) & (col + o < n)
    return jnp.where(keep, rolled, 0.0)


def split(x):
    hi = x.astype(bf16)
    return hi, (x - hi.astype(f32)).astype(bf16)


def make_table(u, tab):
    for v in range(V):
        hl = jnp.concatenate(split(u[0, v, TOP : TOP + NJ, :]), axis=0)
        for e in range(2):
            pick = jnp.where(
                lax.broadcasted_iota(i32, (NK, NK // 2), 0)
                == 2 * lax.broadcasted_iota(i32, (NK, NK // 2), 1) + e,
                1.0,
                0.0,
            ).astype(bf16)
            t = jnp.dot(hl, pick, preferred_element_type=f32)
            parts = [(e, t)]
            if e == 0:
                first = jnp.concatenate([t[1:, :1], jnp.zeros((1, 1), f32)], axis=0)
                parts.append((2, jnp.concatenate([t[:, 1:], first], axis=1)))
            for o, p in parts:
                p = p.astype(bf16)
                tab[pl.ds(160 * o + 32 * v, 32), :] = p[:32]
                tab[pl.ds(480 + 160 * o + 32 * v, 32), :] = p[32:]


def one_hot(base):
    k = (base & (NK - 1)) >> 1
    return jnp.where(lax.broadcasted_iota(i32, (NK // 2, S), 0) == k, 1.0, 0.0).astype(bf16)


def patterns(base, w):
    even = (base & 1) == 0
    row = lax.broadcasted_iota(i32, (NJ, S), 0)
    here, below = row == (base >> 9), row == (base >> 9) + 1
    zero = jnp.zeros_like(w[0])

    def spread(x, y):
        return jnp.where(here, x, jnp.where(below, y, 0.0))

    return (
        spread(jnp.where(even, w[0], zero), jnp.where(even, w[2], zero)),
        spread(jnp.where(even, w[1], w[0]), jnp.where(even, w[3], w[2])),
        spread(jnp.where(even, zero, w[1]), jnp.where(even, zero, w[3])),
    )


def interpolate(tab, hot, ps):
    g = jnp.dot(tab[...], hot, preferred_element_type=f32)
    rows = []
    for v in range(V):
        total = None
        for o in range(3):
            at = 160 * o + 32 * v
            term = (g[at : at + 32] + g[480 + at : 512 + at]) * ps[o]
            total = term if total is None else total + term
        rows.append(jnp.sum(total, axis=0, keepdims=True))
    return jnp.concatenate(rows + [jnp.zeros((3, S), f32)], axis=0)


def kernel(
    blocks,
    field_hbm, source_hbm, inverse_hbm, coupling_hbm, base_hbm, weight_hbm, cell_hbm,
    out,
    source, inverse, coupling, base, weight, cell,
    u, tab, hots, pats, send, recv, acc, frozen, part,
    down_out, up_out, down_in, up_in, const_down_out, const_up_out, const_down_in, const_up_in,
    send_sem, recv_sem, hsend_sem, hrecv_sem, in_sem,
):
    g = lax.axis_index("group")
    b = lax.axis_index("blk")
    groups = blocks // G
    mine, within = b // G, b % G
    other = 1 - g
    is_near = g == 0
    has_low, has_high = b > 0, b < blocks - 1

    def block_rows(ref):
        return ref.at[0, :, pl.ds(TOP, NJ), :]

    loads = [
        pltpu.make_async_copy(a, c, in_sem.at[n])
        for n, (a, c) in enumerate(
            (
                (field_hbm, block_rows(u)),
                (base_hbm, base),
                (weight_hbm, weight),
                (cell_hbm, cell),
                (source_hbm, source.at[:, pl.ds(8, NJ), :]),
                (coupling_hbm, coupling.at[:, pl.ds(8, NJ), :]),
                (inverse_hbm, inverse.at[:, :, pl.ds(8, NJ), :]),
            )
        )
    ]
    for load in loads:
        load.start()

    barrier = pltpu.get_barrier_semaphore()

    def greet(d, c):
        pl.semaphore_signal(barrier, inc=1, device_id=(other, d), device_id_type=MESH)
        return c

    lax.fori_loop(0, blocks, greet, 0)

    for d in ((b + blocks - 1) % blocks, (b + 1) % blocks):
        pl.semaphore_signal(barrier, inc=1, device_id=(g, d), device_id_type=MESH)

    edge_tiles = (slice(0, 8), slice(8 + NJ, 16 + NJ))
    for v in range(V):
        u[0, v, 0:TOP, :] = jnp.zeros((TOP, NK), f32)
        u[0, v, TOP + NJ : 2 * TOP + NJ, :] = jnp.zeros((TOP, NK), f32)
    constants = (
        [(source, (v,)) for v in range(V)]
        + [(inverse, (v, w)) for v in range(V) for w in range(V)]
        + [(coupling, (n,)) for n in range(4)]
    )
    for ref, at in constants + [(frozen, ())]:
        for rows in edge_tiles:
            ref[at + (rows, slice(None))] = jnp.zeros((8, NK), f32)
    for ref in (down_out, up_out, const_down_out, const_up_out):
        ref[...] = jnp.zeros_like(ref)

    for load in loads[:3]:
        load.wait()

    def message(it, i, d):
        return pltpu.make_async_remote_copy(
            src_ref=send.at[d],
            dst_ref=recv.at[it, b],
            send_sem=send_sem,
            recv_sem=recv_sem.at[it, i],
            device_id=(other, d),
            device_id_type=MESH,
        )

    def ship(src, dst, n, direction, slot):
        return pltpu.make_async_remote_copy(
            src_ref=src,
            dst_ref=dst,
            send_sem=hsend_sem.at[n],
            recv_sem=hrecv_sem.at[slot, n],
            device_id=(g, b + direction),
            device_id_type=MESH,
        )

    def edges(it, rows):
        return (
            ship(down_out, down_in.at[it], 0, -1, it),
            ship(up_out.at[pl.ds(0, rows)], up_in.at[it, pl.ds(0, rows)], 1, 1, it),
        )

    def const_edges():
        return (
            ship(const_down_out, const_down_in, 2, -1, 0),
            ship(const_up_out, const_up_in, 3, 1, 0),
        )

    def sweep(it, opening):
        make_table(u, tab)

        def gather_group(i, c):
            dg = (mine + i) % groups
            first = pl.multiple_of(dg * G, G)
            if opening:
                bases = base[pl.ds(first, G), :]
                ws = [weight[q, pl.ds(first, G), :] for q in range(4)]
            for q in range(G):
                if opening:
                    hot = one_hot(bases[q : q + 1])
                    ps = patterns(bases[q : q + 1], [w[q : q + 1] for w in ws])
                    hots[first + q] = hot
                    for o in range(3):
                        pats[first + q, o] = ps[o]
                else:
                    hot = hots[first + q]
                    ps = [pats[first + q, o] for o in range(3)]
                send[first + q] = interpolate(tab, hot, ps)
            if opening:

                @pl.when(i == 0)
                def _():
                    pl.semaphore_wait(barrier, blocks + 2)

            for q in range(G):
                message(it, i, first + (within + q) % G).start()
            return c

        lax.fori_loop(0, groups, gather_group, 0)

        acc[...] = jnp.zeros_like(acc)
        if opening:
            frozen[8 : 8 + NJ, :] = jnp.zeros((NJ, NK), f32)
            for load in loads[3:]:
                load.wait()
            for n, (ref, at) in enumerate(constants):
                const_down_out[2 * n : 2 * n + 2, :] = ref[at + (slice(8, 10), slice(None))]
                const_up_out[3 * n : 3 * n + 3, :] = ref[at + (slice(5 + NJ, 8 + NJ), slice(None))]
            const_down, const_up = const_edges()

            @pl.when(has_low)
            def _():
                const_down.start()

            @pl.when(has_high)
            def _():
                const_up.start()


        def scatter_group(i, c):
            sg = (mine + groups - i) % groups
            first = pl.multiple_of(sg * G, G)
            pltpu.make_async_copy(
                recv.at[it, pl.ds(first, G)], recv.at[it, pl.ds(first, G)], recv_sem.at[it, i]
            ).wait()
            cells = cell[pl.ds(first, G), :]
            left, right = [], []
            for q in range(G):
                r = cells[q : q + 1]
                hit = lax.broadcasted_iota(i32, (NJ, S), 0) == (r >> 9)
                val = recv[it, first + q]
                hi = val.astype(bf16).astype(f32)
                rows = [
                    jnp.where(hit, t[v : v + 1], 0.0) for t in (hi, val - hi) for v in range(V)
                ]
                if opening:
                    rows.append(jnp.where(hit, 1.0, 0.0))
                left.append(jnp.concatenate(rows, axis=0).astype(bf16))
                right.append(
                    jnp.where(
                        lax.broadcasted_iota(i32, (NK, S), 0) == (r & (NK - 1)), 1.0, 0.0
                    ).astype(bf16)
                )
            p = lax.dot_general(
                jnp.concatenate(left, axis=1),
                jnp.concatenate(right, axis=1),
                (((1,), (1,)), ((), ())),
                preferred_element_type=f32,
            )
            acc[...] += p[:320]
            if opening:
                frozen[8 : 8 + NJ, :] += p[320:]
            return c

        lax.fori_loop(0, groups, scatter_group, 0)

        pltpu.make_async_copy(send, send, send_sem).wait()

        fixed = frozen[8 : 8 + NJ, :] > 0.5
        for v in range(V):
            placed = acc[32 * v : 32 * v + 32] + acc[160 + 32 * v : 192 + 32 * v]
            u[0, v, TOP : TOP + NJ, :] = jnp.where(fixed, placed, u[0, v, TOP : TOP + NJ, :])

        for v in range(V):
            down_out[4 * v : 4 * v + 4, :] = u[0, v, TOP : TOP + 4, :]
            up_out[6 * v : 6 * v + 6, :] = u[0, v, TOP + NJ - 6 : TOP + NJ, :]
        if opening:
            down_out[20:22, :] = frozen[8:10, :]
            up_out[30:33, :] = frozen[5 + NJ : 8 + NJ, :]
        down, up = edges(it, 40 if opening else 32)

        @pl.when(has_low)
        def _():
            down.start()

        @pl.when(has_high)
        def _():
            up.start()

        def apply(rows, ts, v):
            return sum(inverse[v, w, rows, :] * ts[w] for w in range(V))

        def near_k(h, v, rows, at):
            x = u[h, v, at : at + 8, :]
            return (
                source[v, rows, :]
                + coupling[2, rows, :] * shift_k(x, -1)
                + coupling[3, rows, :] * shift_k(x, 1)
            )

        def near_rest(h, rows, at, along_k):
            ts = [
                along_k[v]
                + coupling[0, rows, :] * u[h, v, at - 1 : at + 7, :]
                + coupling[1, rows, :] * u[h, v, at + 1 : at + 9, :]
                for v in range(V)
            ]
            parity = (
                lax.broadcasted_iota(i32, (8, NK), 0) + lax.broadcasted_iota(i32, (8, NK), 1)
            ) & 1
            update = (frozen[rows, :] < 0.5) & (parity == h)
            for v in range(V):
                u[1 - h, v, at : at + 8, :] = jnp.where(
                    update, apply(rows, ts, v), u[h, v, at : at + 8, :]
                )

        def off_k(h, v, rows, at):
            x = u[h, v, at : at + 8, :]
            along = sum(a * shift_k(x, o) for o, a in zip(upwind_offsets, upwind_weights))
            return source[v, rows, :] - coupling[1, rows, :] * along

        def off_rest(h, rows, at, along_k):
            ts = []
            for v in range(V):
                along = sum(
                    a * u[h, v, at + o : at + o + 8, :]
                    for o, a in zip(upwind_offsets, upwind_weights)
                )
                ts.append(along_k[v] - coupling[0, rows, :] * along)
            update = frozen[rows, :] < 0.5
            for v in range(V):
                old = u[h, v, at : at + 8, :]
                u[1 - h, v, at : at + 8, :] = jnp.where(update, old + apply(rows, ts, v), old)

        def tile(t):
            return slice(8 * t + 8, 8 * t + 16), TOP + 8 * t

        def before(of_k, rest):
            for t in range(4):
                rows, at = tile(t)
                along_k = [of_k(0, v, rows, at) for v in range(V)]
                if t in (1, 2):
                    rest(0, rows, at, along_k)
                else:
                    for v in range(V):
                        part[v, 8 * t : 8 * t + 8, :] = along_k[v]

        def after(of_k, rest):
            for t in (0, 3):
                rows, at = tile(t)
                rest(0, rows, at, [part[v, 8 * t : 8 * t + 8, :] for v in range(V)])
            for t in (-1, 4):
                rows, at = tile(t)
                rest(0, rows, at, [of_k(0, v, rows, at) for v in range(V)])
            for t in range(4):
                rows, at = tile(t)
                rest(1, rows, at, [of_k(1, v, rows, at) for v in range(V)])

        @pl.when(is_near)
        def _():
            before(near_k, near_rest)

        @pl.when(jnp.logical_not(is_near))
        def _():
            before(off_k, off_rest)

        @pl.when(has_low)
        def _():
            up.wait_recv()
            for v in range(V):
                u[0, v, TOP - 6 : TOP, :] = up_in[it, 6 * v : 6 * v + 6, :]
            if opening:
                frozen[5:8, :] = up_in[it, 30:33, :]
                const_up.wait_recv()
                for n, (ref, at) in enumerate(constants):
                    ref[at + (slice(5, 8), slice(None))] = const_up_in[3 * n : 3 * n + 3, :]

        @pl.when(has_high)
        def _():
            down.wait_recv()
            for v in range(V):
                u[0, v, TOP + NJ : TOP + NJ + 4, :] = down_in[it, 4 * v : 4 * v + 4, :]
            if opening:
                frozen[8 + NJ : 10 + NJ, :] = down_in[it, 20:22, :]
                const_down.wait_recv()
                for n, (ref, at) in enumerate(constants):
                    ref[at + (slice(8 + NJ, 10 + NJ), slice(None))] = const_down_in[2 * n : 2 * n + 2, :]

        @pl.when(is_near)
        def _():
            after(near_k, near_rest)

        @pl.when(jnp.logical_not(is_near))
        def _():
            after(off_k, off_rest)

        @pl.when(has_low)
        def _():
            down.wait_send()
            if opening:
                const_down.wait_send()

        @pl.when(has_high)
        def _():
            up.wait_send()
            if opening:
                const_up.wait_send()

    sweep(0, True)

    def later(it, c):
        sweep(it, False)
        return c

    lax.fori_loop(1, ITERS, later, 0)

    store = pltpu.make_async_copy(block_rows(u), out, in_sem.at[0])
    store.start()
    store.wait()


def on_device(field, source, block_inverse, coupling, donor_base, donor_weight, receiver_cell):
    blocks = donor_base.shape[2]
    hbm = pl.BlockSpec(memory_space=pl.ANY)
    result = pl.pallas_call(
        functools.partial(kernel, blocks),
        out_shape=jax.ShapeDtypeStruct((V, NJ, NK), f32),
        in_specs=[hbm] * 7,
        out_specs=hbm,
        scratch_shapes=[
            pltpu.VMEM((V, NJ + 16, NK), f32),
            pltpu.VMEM((V, V, NJ + 16, NK), f32),
            pltpu.VMEM((4, NJ + 16, NK), f32),
            pltpu.VMEM((blocks, S), i32),
            pltpu.VMEM((4, blocks, S), f32),
            pltpu.VMEM((blocks, S), i32),
            pltpu.VMEM((2, V, 2 * TOP + NJ, NK), f32),
            pltpu.VMEM((960, NK // 2), bf16),
            pltpu.VMEM((blocks, NK // 2, S), bf16),
            pltpu.VMEM((blocks, 3, NJ, S), f32),
            pltpu.VMEM((blocks, 8, S), f32),
            pltpu.VMEM((ITERS, blocks, 8, S), f32),
            pltpu.VMEM((320, NK), f32),
            pltpu.VMEM((NJ + 16, NK), f32),
            pltpu.VMEM((V, NJ, NK), f32),
            pltpu.VMEM((24, NK), f32),
            pltpu.VMEM((40, NK), f32),
            pltpu.VMEM((ITERS, 24, NK), f32),
            pltpu.VMEM((ITERS, 40, NK), f32),
            pltpu.VMEM((72, NK), f32),
            pltpu.VMEM((104, NK), f32),
            pltpu.VMEM((72, NK), f32),
            pltpu.VMEM((104, NK), f32),
            pltpu.SemaphoreType.DMA,
            pltpu.SemaphoreType.DMA((ITERS, blocks // G)),
            pltpu.SemaphoreType.DMA((4,)),
            pltpu.SemaphoreType.DMA((ITERS, 4)),
            pltpu.SemaphoreType.DMA((7,)),
        ],
        compiler_params=pltpu.CompilerParams(
            collective_id=0, has_side_effects=True, vmem_limit_bytes=60 * 2**20
        ),
    )(
        field[0, 0],
        source[0, 0],
        block_inverse[0, 0],
        coupling[0, 0],
        donor_base[0, 0],
        donor_weight[0, 0],
        receiver_cell[0, 0],
    )
    return result[None, None]


def solution(mesh):
    in_specs = (
        P("group", "blk", None, None, None),
        P("group", "blk", None, None, None),
        P("group", "blk", None, None, None, None),
        P("group", "blk", None, None, None),
        P("group", "blk", None, None),
        P("group", "blk", None, None, None),
        P("group", "blk", None, None),
    )
    out_specs = P("group", "blk", None, None, None)
    return jax.shard_map(
        on_device, mesh=mesh, in_specs=in_specs, out_specs=out_specs, check_vma=False
    )
```

```python
import functools

import jax
import jax.numpy as jnp
from jax import lax
from jax.experimental import pallas as pl
from jax.experimental.pallas import tpu as pltpu
from jax.sharding import PartitionSpec as P

ITERS = 4
V = 5
NJ = 32
NK = 512
S = 256
TOP = 16
G = 8

upwind_offsets = (-3, -2, -1, 0, 1, 2)
upwind_weights = (-2.0 / 60.0, 15.0 / 60.0, -60.0 / 60.0, 20.0 / 60.0, 30.0 / 60.0, -3.0 / 60.0)

f32, bf16, i32 = jnp.float32, jnp.bfloat16, jnp.int32
f8 = jnp.float8_e4m3fn
LIFT = 65536.0
MESH = pl.DeviceIdType.MESH


def shift_k(x, o):
    if o == 0:
        return x
    n = x.shape[1]
    col = lax.broadcasted_iota(i32, x.shape, 1)
    rolled = pltpu.roll(x, (-o) % n, axis=1)
    keep = (col + o >= 0) & (col + o < n)
    return jnp.where(keep, rolled, 0.0)


def split(x):
    hi = x.astype(bf16)
    return hi, (x - hi.astype(f32)).astype(bf16)


def largest(x):
    m = jnp.max(jnp.max(jnp.abs(x), axis=1, keepdims=True), axis=0, keepdims=True)
    return jnp.maximum(m, 1e-30)


def swap_columns(inverse):
    a = lax.broadcasted_iota(i32, (NK, NK), 1 if inverse else 0)
    c = lax.broadcasted_iota(i32, (NK, NK), 0 if inverse else 1)
    return jnp.where(a == 2 * (c & (NK // 2 - 1)) + (c >> 8), 1.0, 0.0).astype(bf16)


def make_table(u, tab, tab8, pick):
    a = jnp.concatenate([u[0, v, TOP : TOP + NJ, :] for v in range(V)], axis=0)
    m = largest(a)
    t = jnp.dot(
        jnp.concatenate(split(a * (LIFT / m)), axis=0), pick[...], preferred_element_type=f32
    )
    t0, t1 = t[:, : NK // 2], t[:, NK // 2 :]
    first = jnp.concatenate([t0[1:, :1], jnp.zeros((1, 1), f32)], axis=0)
    t2 = jnp.concatenate([t0[:, 1:], first], axis=1)
    for o, p in enumerate((t0, t1, t2)):
        tab[pl.ds(160 * o, 160), :] = p[:160].astype(bf16)
        tab8[pl.ds(160 * o, 160), :] = p[160:].astype(f8)
    return m * (1.0 / LIFT)


def one_hot(base):
    k = (base & (NK - 1)) >> 1
    return jnp.where(lax.broadcasted_iota(i32, (NK // 2, S), 0) == k, 1.0, 0.0)


def patterns(base, w):
    even = (base & 1) == 0
    row = lax.broadcasted_iota(i32, (NJ, S), 0)
    here, below = row == (base >> 9), row == (base >> 9) + 1
    zero = jnp.zeros_like(w[0])

    def spread(x, y):
        return jnp.where(here, x, jnp.where(below, y, 0.0))

    return (
        spread(jnp.where(even, w[0], zero), jnp.where(even, w[2], zero)),
        spread(jnp.where(even, w[1], w[0]), jnp.where(even, w[3], w[2])),
        spread(jnp.where(even, zero, w[1]), jnp.where(even, zero, w[3])),
    )


def interpolate(tab, tab8, hot, hot8, ps, undo):
    high = jnp.dot(tab[...], hot, preferred_element_type=f32)
    low = jnp.dot(tab8[...], hot8, preferred_element_type=f32)
    rows = []
    for v in range(V):
        total = None
        for o in range(3):
            at = 160 * o + 32 * v
            term = (high[at : at + 32] + low[at : at + 32]) * ps[o]
            total = term if total is None else total + term
        rows.append(jnp.sum(total, axis=0, keepdims=True))
    return jnp.concatenate(rows + [jnp.zeros((3, S), f32)], axis=0) * undo


def rows_of(half):
    r = lax.broadcasted_iota(i32, (16, S), 0)
    return r + 8 if half else jnp.where(r < 8, r, r + 16)


def kernel(
    blocks,
    field_hbm, source_hbm, inverse_hbm, coupling_hbm, base_hbm, weight_hbm, cell_hbm,
    out,
    source, inverse, coupling, base, weight, cell,
    u, tab, tab8, pick, spread, hots, hots8, pats, cell_hots, cell_hots8,
    send, recv, acc, marks, frozen, part,
    down_out, up_out, down_in, up_in, const_down_out, const_up_out, const_down_in, const_up_in,
    send_sem, recv_sem, hsend_sem, hrecv_sem, in_sem,
):
    g = lax.axis_index("group")
    b = lax.axis_index("blk")
    groups = blocks // G
    mine, within = b // G, b % G
    other = 1 - g
    is_near = g == 0
    has_low, has_high = b > 0, b < blocks - 1

    def block_rows(ref):
        return ref.at[0, :, pl.ds(TOP, NJ), :]

    loads = [
        pltpu.make_async_copy(a, c, in_sem.at[n])
        for n, (a, c) in enumerate(
            (
                (field_hbm, block_rows(u)),
                (base_hbm, base),
                (weight_hbm, weight),
                (cell_hbm, cell),
                (source_hbm, source.at[:, pl.ds(8, NJ), :]),
                (coupling_hbm, coupling.at[:, pl.ds(8, NJ), :]),
                (inverse_hbm, inverse.at[:, :, pl.ds(8, NJ), :]),
            )
        )
    ]
    for load in loads:
        load.start()

    barrier = pltpu.get_barrier_semaphore()

    def greet(d, c):
        pl.semaphore_signal(barrier, inc=1, device_id=(other, d), device_id_type=MESH)
        return c

    lax.fori_loop(0, blocks, greet, 0)

    for d in ((b + blocks - 1) % blocks, (b + 1) % blocks):
        pl.semaphore_signal(barrier, inc=1, device_id=(g, d), device_id_type=MESH)

    edge_tiles = (slice(0, 8), slice(8 + NJ, 16 + NJ))
    for v in range(V):
        u[0, v, 0:TOP, :] = jnp.zeros((TOP, NK), f32)
        u[0, v, TOP + NJ : 2 * TOP + NJ, :] = jnp.zeros((TOP, NK), f32)
    constants = (
        [(source, (v,)) for v in range(V)]
        + [(inverse, (v, w)) for v in range(V) for w in range(V)]
        + [(coupling, (n,)) for n in range(4)]
    )
    for ref, at in constants + [(frozen, ())]:
        for rows in edge_tiles:
            ref[at + (rows, slice(None))] = jnp.zeros((8, NK), f32)
    for ref in (down_out, up_out, const_down_out, const_up_out):
        ref[...] = jnp.zeros_like(ref)

    pick[...] = swap_columns(False)
    spread[...] = swap_columns(True)

    for load in loads[:3]:
        load.wait()

    def message(it, i, d):
        return pltpu.make_async_remote_copy(
            src_ref=send.at[d],
            dst_ref=recv.at[it, b],
            send_sem=send_sem,
            recv_sem=recv_sem.at[it, i],
            device_id=(other, d),
            device_id_type=MESH,
        )

    def ship(src, dst, n, direction, slot):
        return pltpu.make_async_remote_copy(
            src_ref=src,
            dst_ref=dst,
            send_sem=hsend_sem.at[n],
            recv_sem=hrecv_sem.at[slot, n],
            device_id=(g, b + direction),
            device_id_type=MESH,
        )

    def edges(it, rows):
        return (
            ship(down_out, down_in.at[it], 0, -1, it),
            ship(up_out.at[pl.ds(0, rows)], up_in.at[it, pl.ds(0, rows)], 1, 1, it),
        )

    def const_edges():
        return (
            ship(const_down_out, const_down_in, 2, -1, 0),
            ship(const_up_out, const_up_in, 3, 1, 0),
        )

    def sweep(it, opening):
        undo = make_table(u, tab, tab8, pick)

        def gather_group(i, c):
            dg = (mine + i) % groups
            first = pl.multiple_of(dg * G, G)
            if opening:
                bases = base[pl.ds(first, G), :]
                ws = [weight[q, pl.ds(first, G), :] for q in range(4)]
            for q in range(G):
                if opening:
                    hot = one_hot(bases[q : q + 1])
                    hot, hot8 = hot.astype(bf16), hot.astype(f8)
                    ps = patterns(bases[q : q + 1], [w[q : q + 1] for w in ws])
                    hots[first + q] = hot
                    hots8[first + q] = hot8
                    for o in range(3):
                        pats[first + q, o] = ps[o]
                else:
                    hot, hot8 = hots[first + q], hots8[first + q]
                    ps = [pats[first + q, o] for o in range(3)]
                send[first + q] = interpolate(tab, tab8, hot, hot8, ps, undo)
            if opening:

                @pl.when(i == 0)
                def _():
                    pl.semaphore_wait(barrier, blocks + 2)

            for q in range(G):
                message(it, i, first + (within + q) % G).start()
            return c

        lax.fori_loop(0, groups, gather_group, 0)

        if opening:
            for load in loads[3:]:
                load.wait()
            for n, (ref, at) in enumerate(constants):
                const_down_out[2 * n : 2 * n + 2, :] = ref[at + (slice(8, 10), slice(None))]
                const_up_out[3 * n : 3 * n + 3, :] = ref[at + (slice(5 + NJ, 8 + NJ), slice(None))]
            const_down, const_up = const_edges()

            @pl.when(has_low)
            def _():
                const_down.start()

            @pl.when(has_high)
            def _():
                const_up.start()


        def scatter_group(i, c, half):
            sg = (mine + groups - i) % groups
            first = pl.multiple_of(sg * G, G)
            if not half:
                pltpu.make_async_copy(
                    recv.at[it, pl.ds(first, G)], recv.at[it, pl.ds(first, G)], recv_sem.at[it, i]
                ).wait()
            cells = cell[pl.ds(first, G), :]
            slots = pl.ds(pl.multiple_of(first * S, S), G * S)
            if opening and not half:
                down_cells = jnp.transpose(cells.astype(f32)).astype(i32)
                for q in range(G):
                    hot = jnp.where(
                        lax.broadcasted_iota(i32, (S, NK // 2), 1)
                        == (down_cells[:, q : q + 1] & (NK - 1)) >> 1,
                        1.0,
                        0.0,
                    )
                    at = pl.ds(pl.multiple_of((first + q) * S, S), S)
                    cell_hots[at, :] = hot.astype(bf16)
                    cell_hots8[at, :] = hot.astype(f8)
            vals = [recv[it, first + q] for q in range(G)]
            m = largest(functools.reduce(jnp.maximum, [jnp.abs(x) for x in vals]))
            scale = LIFT / m
            highs, lows = [], []
            for q in range(G):
                r = cells[q : q + 1]
                hit = rows_of(half) == (r >> 9)
                even = (r & 1) == 0
                hits = (hit & even, hit & jnp.logical_not(even))
                high = vals[q].astype(bf16).astype(f32)
                low = (vals[q] - high) * scale
                rows = [jnp.where(x, high[v : v + 1], 0.0) for x in hits for v in range(V)]
                if opening:
                    rows += [jnp.where(x, 1.0, 0.0) for x in hits]
                highs.append(jnp.concatenate(rows, axis=0).astype(bf16))
                rows = [jnp.where(x, low[v : v + 1], 0.0) for x in hits for v in range(V)]
                lows.append(jnp.concatenate(rows, axis=0).astype(f8))
            p = jnp.dot(
                jnp.concatenate(highs, axis=1), cell_hots[slots, :], preferred_element_type=f32
            )
            acc[0] += p[:160]
            if opening:
                marks[...] += p[160:]
            p = jnp.dot(
                jnp.concatenate(lows, axis=1), cell_hots8[slots, :], preferred_element_type=f32
            )
            acc[1] += p * (m * (1.0 / LIFT))
            return c

        def interleave(even, odd):
            pair = jnp.concatenate([even, odd], axis=1).astype(bf16)
            return jnp.dot(pair, spread[...], preferred_element_type=f32)

        def place(half):
            acc[...] = jnp.zeros_like(acc)
            if opening:
                marks[...] = jnp.zeros_like(marks)
            lax.fori_loop(0, groups, functools.partial(scatter_group, half=half), 0)
            placed = interleave(acc[0, :80, :], acc[0, 80:, :]) + interleave(acc[1, :80, :], acc[1, 80:, :])
            pieces = ((0, 8), (8, 16)) if half else ((0, 0), (8, 24))
            if opening:
                mark = interleave(marks[:16, :], marks[16:, :])
            for n, j in pieces:
                if opening:
                    frozen[8 + j : 16 + j, :] = mark[n : n + 8]
                fixed = frozen[8 + j : 16 + j, :] > 0.5
                for v in range(V):
                    at = TOP + j
                    u[0, v, at : at + 8, :] = jnp.where(
                        fixed, placed[16 * v + n : 16 * v + n + 8], u[0, v, at : at + 8, :]
                    )

        place(0)

        for v in range(V):
            down_out[4 * v : 4 * v + 4, :] = u[0, v, TOP : TOP + 4, :]
            up_out[6 * v : 6 * v + 6, :] = u[0, v, TOP + NJ - 6 : TOP + NJ, :]
        if opening:
            down_out[20:22, :] = frozen[8:10, :]
            up_out[30:33, :] = frozen[5 + NJ : 8 + NJ, :]
        down, up = edges(it, 40 if opening else 32)

        @pl.when(has_low)
        def _():
            down.start()

        @pl.when(has_high)
        def _():
            up.start()

        place(1)

        pltpu.make_async_copy(send, send, send_sem).wait()

        def apply(rows, ts, v):
            return sum(inverse[v, w, rows, :] * ts[w] for w in range(V))

        def near_k(h, v, rows, at):
            x = u[h, v, at : at + 8, :]
            return (
                source[v, rows, :]
                + coupling[2, rows, :] * shift_k(x, -1)
                + coupling[3, rows, :] * shift_k(x, 1)
            )

        def near_rest(h, rows, at, along_k):
            ts = [
                along_k[v]
                + coupling[0, rows, :] * u[h, v, at - 1 : at + 7, :]
                + coupling[1, rows, :] * u[h, v, at + 1 : at + 9, :]
                for v in range(V)
            ]
            parity = (
                lax.broadcasted_iota(i32, (8, NK), 0) + lax.broadcasted_iota(i32, (8, NK), 1)
            ) & 1
            update = (frozen[rows, :] < 0.5) & (parity == h)
            for v in range(V):
                u[1 - h, v, at : at + 8, :] = jnp.where(
                    update, apply(rows, ts, v), u[h, v, at : at + 8, :]
                )

        def off_k(h, v, rows, at):
            x = u[h, v, at : at + 8, :]
            along = sum(a * shift_k(x, o) for o, a in zip(upwind_offsets, upwind_weights))
            return source[v, rows, :] - coupling[1, rows, :] * along

        def off_rest(h, rows, at, along_k):
            ts = []
            for v in range(V):
                along = sum(
                    a * u[h, v, at + o : at + o + 8, :]
                    for o, a in zip(upwind_offsets, upwind_weights)
                )
                ts.append(along_k[v] - coupling[0, rows, :] * along)
            update = frozen[rows, :] < 0.5
            for v in range(V):
                old = u[h, v, at : at + 8, :]
                u[1 - h, v, at : at + 8, :] = jnp.where(update, old + apply(rows, ts, v), old)

        def tile(t):
            return slice(8 * t + 8, 8 * t + 16), TOP + 8 * t

        def before(of_k, rest):
            for t in range(4):
                rows, at = tile(t)
                along_k = [of_k(0, v, rows, at) for v in range(V)]
                if t in (1, 2):
                    rest(0, rows, at, along_k)
                else:
                    for v in range(V):
                        part[v, 8 * t : 8 * t + 8, :] = along_k[v]

        def after(of_k, rest):
            for t in (0, 3):
                rows, at = tile(t)
                rest(0, rows, at, [part[v, 8 * t : 8 * t + 8, :] for v in range(V)])
            for t in (-1, 4):
                rows, at = tile(t)
                rest(0, rows, at, [of_k(0, v, rows, at) for v in range(V)])
            for t in range(4):
                rows, at = tile(t)
                rest(1, rows, at, [of_k(1, v, rows, at) for v in range(V)])

        @pl.when(is_near)
        def _():
            before(near_k, near_rest)

        @pl.when(jnp.logical_not(is_near))
        def _():
            before(off_k, off_rest)

        @pl.when(has_low)
        def _():
            up.wait_recv()
            for v in range(V):
                u[0, v, TOP - 6 : TOP, :] = up_in[it, 6 * v : 6 * v + 6, :]
            if opening:
                frozen[5:8, :] = up_in[it, 30:33, :]
                const_up.wait_recv()
                for n, (ref, at) in enumerate(constants):
                    ref[at + (slice(5, 8), slice(None))] = const_up_in[3 * n : 3 * n + 3, :]

        @pl.when(has_high)
        def _():
            down.wait_recv()
            for v in range(V):
                u[0, v, TOP + NJ : TOP + NJ + 4, :] = down_in[it, 4 * v : 4 * v + 4, :]
            if opening:
                frozen[8 + NJ : 10 + NJ, :] = down_in[it, 20:22, :]
                const_down.wait_recv()
                for n, (ref, at) in enumerate(constants):
                    ref[at + (slice(8 + NJ, 10 + NJ), slice(None))] = const_down_in[2 * n : 2 * n + 2, :]

        @pl.when(is_near)
        def _():
            after(near_k, near_rest)

        @pl.when(jnp.logical_not(is_near))
        def _():
            after(off_k, off_rest)

        @pl.when(has_low)
        def _():
            down.wait_send()
            if opening:
                const_down.wait_send()

        @pl.when(has_high)
        def _():
            up.wait_send()
            if opening:
                const_up.wait_send()

    sweep(0, True)

    def later(it, c):
        sweep(it, False)
        return c

    lax.fori_loop(1, ITERS, later, 0)

    store = pltpu.make_async_copy(block_rows(u), out, in_sem.at[0])
    store.start()
    store.wait()


def on_device(field, source, block_inverse, coupling, donor_base, donor_weight, receiver_cell):
    blocks = donor_base.shape[2]
    hbm = pl.BlockSpec(memory_space=pl.ANY)
    result = pl.pallas_call(
        functools.partial(kernel, blocks),
        out_shape=jax.ShapeDtypeStruct((V, NJ, NK), f32),
        in_specs=[hbm] * 7,
        out_specs=hbm,
        scratch_shapes=[
            pltpu.VMEM((V, NJ + 16, NK), f32),
            pltpu.VMEM((V, V, NJ + 16, NK), f32),
            pltpu.VMEM((4, NJ + 16, NK), f32),
            pltpu.VMEM((blocks, S), i32),
            pltpu.VMEM((4, blocks, S), f32),
            pltpu.VMEM((blocks, S), i32),
            pltpu.VMEM((2, V, 2 * TOP + NJ, NK), f32),
            pltpu.VMEM((480, NK // 2), bf16),
            pltpu.VMEM((480, NK // 2), f8),
            pltpu.VMEM((NK, NK), bf16),
            pltpu.VMEM((NK, NK), bf16),
            pltpu.VMEM((blocks, NK // 2, S), bf16),
            pltpu.VMEM((blocks, NK // 2, S), f8),
            pltpu.VMEM((blocks, 3, NJ, S), f32),
            pltpu.VMEM((blocks * S, NK // 2), bf16),
            pltpu.VMEM((blocks * S, NK // 2), f8),
            pltpu.VMEM((blocks, 8, S), f32),
            pltpu.VMEM((ITERS, blocks, 8, S), f32),
            pltpu.VMEM((2, 160, NK // 2), f32),
            pltpu.VMEM((32, NK // 2), f32),
            pltpu.VMEM((NJ + 16, NK), f32),
            pltpu.VMEM((V, NJ, NK), f32),
            pltpu.VMEM((24, NK), f32),
            pltpu.VMEM((40, NK), f32),
            pltpu.VMEM((ITERS, 24, NK), f32),
            pltpu.VMEM((ITERS, 40, NK), f32),
            pltpu.VMEM((72, NK), f32),
            pltpu.VMEM((104, NK), f32),
            pltpu.VMEM((72, NK), f32),
            pltpu.VMEM((104, NK), f32),
            pltpu.SemaphoreType.DMA,
            pltpu.SemaphoreType.DMA((ITERS, blocks // G)),
            pltpu.SemaphoreType.DMA((4,)),
            pltpu.SemaphoreType.DMA((ITERS, 4)),
            pltpu.SemaphoreType.DMA((7,)),
        ],
        compiler_params=pltpu.CompilerParams(
            collective_id=0, has_side_effects=True, vmem_limit_bytes=60 * 2**20
        ),
    )(
        field[0, 0],
        source[0, 0],
        block_inverse[0, 0],
        coupling[0, 0],
        donor_base[0, 0],
        donor_weight[0, 0],
        receiver_cell[0, 0],
    )
    return result[None, None]


def solution(mesh):
    in_specs = (
        P("group", "blk", None, None, None),
        P("group", "blk", None, None, None),
        P("group", "blk", None, None, None, None),
        P("group", "blk", None, None, None),
        P("group", "blk", None, None),
        P("group", "blk", None, None, None),
        P("group", "blk", None, None),
    )
    out_specs = P("group", "blk", None, None, None)
    return jax.shard_map(
        on_device, mesh=mesh, in_specs=in_specs, out_specs=out_specs, check_vma=False
    )
```

```python
import functools

import jax
import jax.numpy as jnp
from jax import lax
from jax.experimental import pallas as pl
from jax.experimental.pallas import tpu as pltpu
from jax.sharding import PartitionSpec as P

ITERS = 4
V = 5
NJ = 32
NK = 512
S = 256
TOP = 16
G = 8

upwind_offsets = (-3, -2, -1, 0, 1, 2)
upwind_weights = (-2.0 / 60.0, 15.0 / 60.0, -60.0 / 60.0, 20.0 / 60.0, 30.0 / 60.0, -3.0 / 60.0)

f32, bf16, i32 = jnp.float32, jnp.bfloat16, jnp.int32
f8 = jnp.float8_e4m3fn
LIFT = 65536.0
MESH = pl.DeviceIdType.MESH


def shift_k(x, o):
    if o == 0:
        return x
    n = x.shape[1]
    col = lax.broadcasted_iota(i32, x.shape, 1)
    rolled = pltpu.roll(x, (-o) % n, axis=1)
    keep = (col + o >= 0) & (col + o < n)
    return jnp.where(keep, rolled, 0.0)


def split(x):
    hi = x.astype(bf16)
    return hi, (x - hi.astype(f32)).astype(bf16)


def largest(x):
    m = jnp.max(jnp.max(jnp.abs(x), axis=1, keepdims=True), axis=0, keepdims=True)
    return jnp.maximum(m, 1e-30)


def swap_columns(inverse):
    a = lax.broadcasted_iota(i32, (NK, NK), 1 if inverse else 0)
    c = lax.broadcasted_iota(i32, (NK, NK), 0 if inverse else 1)
    return jnp.where(a == 2 * (c & (NK // 2 - 1)) + (c >> 8), 1.0, 0.0).astype(bf16)


def make_table(u, tab, tab8, pick):
    a = jnp.concatenate([u[0, v, TOP : TOP + NJ, :] for v in range(V)], axis=0)
    m = largest(a)
    t = jnp.dot(
        jnp.concatenate(split(a * (LIFT / m)), axis=0), pick[...], preferred_element_type=f32
    )
    t0, t1 = t[:, : NK // 2], t[:, NK // 2 :]
    first = jnp.concatenate([t0[1:, :1], jnp.zeros((1, 1), f32)], axis=0)
    t2 = jnp.concatenate([t0[:, 1:], first], axis=1)
    for o, p in enumerate((t0, t1, t2)):
        tab[pl.ds(160 * o, 160), :] = p[:160].astype(bf16)
        tab8[pl.ds(160 * o, 160), :] = p[160:].astype(f8)
    return m * (1.0 / LIFT)


def one_hot(base):
    k = (base & (NK - 1)) >> 1
    return jnp.where(lax.broadcasted_iota(i32, (NK // 2, S), 0) == k, 1.0, 0.0)


def patterns(base, w):
    even = (base & 1) == 0
    row = lax.broadcasted_iota(i32, (NJ, S), 0)
    here, below = row == (base >> 9), row == (base >> 9) + 1
    zero = jnp.zeros_like(w[0])

    def spread(x, y):
        return jnp.where(here, x, jnp.where(below, y, 0.0))

    return (
        spread(jnp.where(even, w[0], zero), jnp.where(even, w[2], zero)),
        spread(jnp.where(even, w[1], w[0]), jnp.where(even, w[3], w[2])),
        spread(jnp.where(even, zero, w[1]), jnp.where(even, zero, w[3])),
    )


def interpolate(tab, tab8, hot, hot8, ps, undo):
    high = jnp.dot(tab[...], hot, preferred_element_type=f32)
    low = jnp.dot(tab8[...], hot8, preferred_element_type=f32)
    rows = []
    for v in range(V):
        total = None
        for o in range(3):
            at = 160 * o + 32 * v
            term = (high[at : at + 32] + low[at : at + 32]) * ps[o]
            total = term if total is None else total + term
        rows.append(jnp.sum(total, axis=0, keepdims=True))
    return jnp.concatenate(rows + [jnp.zeros((3, S), f32)], axis=0) * undo


def rows_of(half):
    r = lax.broadcasted_iota(i32, (16, S), 0)
    return r + 8 if half else jnp.where(r < 8, r, r + 16)


def kernel(
    blocks,
    field_hbm, source_hbm, inverse_hbm, coupling_hbm, base_hbm, weight_hbm, cell_hbm,
    out,
    source, inverse, coupling, base, weight, cell,
    u, tab, tab8, pick, spread, hots, hots8, pats, cell_hots, cell_hots8,
    send, recv, acc, marks, frozen, part,
    down_out, up_out, down_in, up_in, const_down_out, const_up_out, const_down_in, const_up_in,
    send_sem, recv_sem, hsend_sem, hrecv_sem, in_sem,
):
    g = lax.axis_index("group")
    b = lax.axis_index("blk")
    groups = blocks // G
    mine, within = b // G, b % G
    other = 1 - g
    is_near = g == 0
    has_low, has_high = b > 0, b < blocks - 1

    def block_rows(ref):
        return ref.at[0, :, pl.ds(TOP, NJ), :]

    loads = [
        pltpu.make_async_copy(a, c, in_sem.at[n])
        for n, (a, c) in enumerate(
            (
                (field_hbm, block_rows(u)),
                (base_hbm, base),
                (weight_hbm, weight),
                (cell_hbm, cell),
                (source_hbm, source.at[:, pl.ds(8, NJ), :]),
                (coupling_hbm, coupling.at[:, pl.ds(8, NJ), :]),
                (inverse_hbm, inverse.at[:, :, pl.ds(8, NJ), :]),
            )
        )
    ]
    for load in loads:
        load.start()

    barrier = pltpu.get_barrier_semaphore()

    def greet(d, c):
        pl.semaphore_signal(barrier, inc=1, device_id=(other, d), device_id_type=MESH)
        return c

    lax.fori_loop(0, blocks, greet, 0)

    for d in ((b + blocks - 1) % blocks, (b + 1) % blocks):
        pl.semaphore_signal(barrier, inc=1, device_id=(g, d), device_id_type=MESH)

    edge_tiles = (slice(0, 8), slice(8 + NJ, 16 + NJ))
    for v in range(V):
        u[0, v, 0:TOP, :] = jnp.zeros((TOP, NK), f32)
        u[0, v, TOP + NJ : 2 * TOP + NJ, :] = jnp.zeros((TOP, NK), f32)
    constants = (
        [(source, (v,)) for v in range(V)]
        + [(inverse, (v, w)) for v in range(V) for w in range(V)]
        + [(coupling, (n,)) for n in range(4)]
    )
    for ref, at in constants + [(frozen, ())]:
        for rows in edge_tiles:
            ref[at + (rows, slice(None))] = jnp.zeros((8, NK), f32)
    for ref in (down_out, up_out, const_down_out, const_up_out):
        ref[...] = jnp.zeros_like(ref)

    pick[...] = swap_columns(False)
    spread[...] = swap_columns(True)

    for load in loads[:3]:
        load.wait()

    def far_first(turn):
        return groups // 2 + ((turn + 1) // 2) * (1 - 2 * (turn % 2))

    def message(it, i, d):
        return pltpu.make_async_remote_copy(
            src_ref=send.at[d],
            dst_ref=recv.at[it, b],
            send_sem=send_sem,
            recv_sem=recv_sem.at[it, i],
            device_id=(other, d),
            device_id_type=MESH,
        )

    def ship(src, dst, n, direction, slot):
        return pltpu.make_async_remote_copy(
            src_ref=src,
            dst_ref=dst,
            send_sem=hsend_sem.at[n],
            recv_sem=hrecv_sem.at[slot, n],
            device_id=(g, b + direction),
            device_id_type=MESH,
        )

    def edges(it, rows):
        return (
            ship(down_out, down_in.at[it], 0, -1, it),
            ship(up_out.at[pl.ds(0, rows)], up_in.at[it, pl.ds(0, rows)], 1, 1, it),
        )

    def const_edges():
        return (
            ship(const_down_out, const_down_in, 2, -1, 0),
            ship(const_up_out, const_up_in, 3, 1, 0),
        )

    def sweep(it, opening):
        undo = make_table(u, tab, tab8, pick)

        def gather_group(turn, c):
            i = far_first(turn)
            dg = (mine + i) % groups
            first = pl.multiple_of(dg * G, G)
            if opening:
                bases = base[pl.ds(first, G), :]
                ws = [weight[q, pl.ds(first, G), :] for q in range(4)]
            for q in range(G):
                if opening:
                    hot = one_hot(bases[q : q + 1])
                    hot, hot8 = hot.astype(bf16), hot.astype(f8)
                    ps = patterns(bases[q : q + 1], [w[q : q + 1] for w in ws])
                    hots[first + q] = hot
                    hots8[first + q] = hot8
                    for o in range(3):
                        pats[first + q, o] = ps[o]
                else:
                    hot, hot8 = hots[first + q], hots8[first + q]
                    ps = [pats[first + q, o] for o in range(3)]
                send[first + q] = interpolate(tab, tab8, hot, hot8, ps, undo)
            if opening:

                @pl.when(turn == 0)
                def _():
                    pl.semaphore_wait(barrier, blocks + 2)

            for q in range(G):
                message(it, i, first + (within + q) % G).start()
            return c

        lax.fori_loop(0, groups, gather_group, 0)

        if opening:
            for load in loads[3:]:
                load.wait()
            for n, (ref, at) in enumerate(constants):
                const_down_out[2 * n : 2 * n + 2, :] = ref[at + (slice(8, 10), slice(None))]
                const_up_out[3 * n : 3 * n + 3, :] = ref[at + (slice(5 + NJ, 8 + NJ), slice(None))]
            const_down, const_up = const_edges()

            @pl.when(has_low)
            def _():
                const_down.start()

            @pl.when(has_high)
            def _():
                const_up.start()


        def scatter_group(turn, c, half):
            i = far_first(turn)
            sg = (mine + groups - i) % groups
            first = pl.multiple_of(sg * G, G)
            if not half:
                pltpu.make_async_copy(
                    recv.at[it, pl.ds(first, G)], recv.at[it, pl.ds(first, G)], recv_sem.at[it, i]
                ).wait()
            cells = cell[pl.ds(first, G), :]
            slots = pl.ds(pl.multiple_of(first * S, S), G * S)
            if opening and not half:
                down_cells = jnp.transpose(cells.astype(f32)).astype(i32)
                for q in range(G):
                    hot = jnp.where(
                        lax.broadcasted_iota(i32, (S, NK // 2), 1)
                        == (down_cells[:, q : q + 1] & (NK - 1)) >> 1,
                        1.0,
                        0.0,
                    )
                    at = pl.ds(pl.multiple_of((first + q) * S, S), S)
                    cell_hots[at, :] = hot.astype(bf16)
                    cell_hots8[at, :] = hot.astype(f8)
            vals = [recv[it, first + q] for q in range(G)]
            m = largest(functools.reduce(jnp.maximum, [jnp.abs(x) for x in vals]))
            scale = LIFT / m
            highs, lows = [], []
            for q in range(G):
                r = cells[q : q + 1]
                hit = rows_of(half) == (r >> 9)
                even = (r & 1) == 0
                hits = (hit & even, hit & jnp.logical_not(even))
                high = vals[q].astype(bf16).astype(f32)
                low = (vals[q] - high) * scale
                rows = [jnp.where(x, high[v : v + 1], 0.0) for x in hits for v in range(V)]
                if opening:
                    rows += [jnp.where(x, 1.0, 0.0) for x in hits]
                highs.append(jnp.concatenate(rows, axis=0).astype(bf16))
                rows = [jnp.where(x, low[v : v + 1], 0.0) for x in hits for v in range(V)]
                lows.append(jnp.concatenate(rows, axis=0).astype(f8))
            p = jnp.dot(
                jnp.concatenate(highs, axis=1), cell_hots[slots, :], preferred_element_type=f32
            )
            acc[0] += p[:160]
            if opening:
                marks[...] += p[160:]
            p = jnp.dot(
                jnp.concatenate(lows, axis=1), cell_hots8[slots, :], preferred_element_type=f32
            )
            acc[1] += p * (m * (1.0 / LIFT))
            return c

        def interleave(even, odd):
            pair = jnp.concatenate([even, odd], axis=1).astype(bf16)
            return jnp.dot(pair, spread[...], preferred_element_type=f32)

        def place(half):
            acc[...] = jnp.zeros_like(acc)
            if opening:
                marks[...] = jnp.zeros_like(marks)
            lax.fori_loop(0, groups, functools.partial(scatter_group, half=half), 0)
            placed = interleave(acc[0, :80, :], acc[0, 80:, :]) + interleave(acc[1, :80, :], acc[1, 80:, :])
            pieces = ((0, 8), (8, 16)) if half else ((0, 0), (8, 24))
            if opening:
                mark = interleave(marks[:16, :], marks[16:, :])
            for n, j in pieces:
                if opening:
                    frozen[8 + j : 16 + j, :] = mark[n : n + 8]
                fixed = frozen[8 + j : 16 + j, :] > 0.5
                for v in range(V):
                    at = TOP + j
                    u[0, v, at : at + 8, :] = jnp.where(
                        fixed, placed[16 * v + n : 16 * v + n + 8], u[0, v, at : at + 8, :]
                    )

        place(0)

        for v in range(V):
            down_out[4 * v : 4 * v + 4, :] = u[0, v, TOP : TOP + 4, :]
            up_out[6 * v : 6 * v + 6, :] = u[0, v, TOP + NJ - 6 : TOP + NJ, :]
        if opening:
            down_out[20:22, :] = frozen[8:10, :]
            up_out[30:33, :] = frozen[5 + NJ : 8 + NJ, :]
        down, up = edges(it, 40 if opening else 32)

        @pl.when(has_low)
        def _():
            down.start()

        @pl.when(has_high)
        def _():
            up.start()

        place(1)

        pltpu.make_async_copy(send, send, send_sem).wait()

        def apply(rows, ts, v):
            return sum(inverse[v, w, rows, :] * ts[w] for w in range(V))

        def near_k(h, v, rows, at):
            x = u[h, v, at : at + 8, :]
            return (
                source[v, rows, :]
                + coupling[2, rows, :] * shift_k(x, -1)
                + coupling[3, rows, :] * shift_k(x, 1)
            )

        def near_rest(h, rows, at, along_k):
            ts = [
                along_k[v]
                + coupling[0, rows, :] * u[h, v, at - 1 : at + 7, :]
                + coupling[1, rows, :] * u[h, v, at + 1 : at + 9, :]
                for v in range(V)
            ]
            parity = (
                lax.broadcasted_iota(i32, (8, NK), 0) + lax.broadcasted_iota(i32, (8, NK), 1)
            ) & 1
            update = (frozen[rows, :] < 0.5) & (parity == h)
            for v in range(V):
                u[1 - h, v, at : at + 8, :] = jnp.where(
                    update, apply(rows, ts, v), u[h, v, at : at + 8, :]
                )

        def off_k(h, v, rows, at):
            x = u[h, v, at : at + 8, :]
            along = sum(a * shift_k(x, o) for o, a in zip(upwind_offsets, upwind_weights))
            return source[v, rows, :] - coupling[1, rows, :] * along

        def off_rest(h, rows, at, along_k):
            ts = []
            for v in range(V):
                along = sum(
                    a * u[h, v, at + o : at + o + 8, :]
                    for o, a in zip(upwind_offsets, upwind_weights)
                )
                ts.append(along_k[v] - coupling[0, rows, :] * along)
            update = frozen[rows, :] < 0.5
            for v in range(V):
                old = u[h, v, at : at + 8, :]
                u[1 - h, v, at : at + 8, :] = jnp.where(update, old + apply(rows, ts, v), old)

        def tile(t):
            return slice(8 * t + 8, 8 * t + 16), TOP + 8 * t

        def before(of_k, rest):
            for t in range(4):
                rows, at = tile(t)
                along_k = [of_k(0, v, rows, at) for v in range(V)]
                if t in (1, 2):
                    rest(0, rows, at, along_k)
                else:
                    for v in range(V):
                        part[v, 8 * t : 8 * t + 8, :] = along_k[v]

        def after(of_k, rest):
            for t in (0, 3):
                rows, at = tile(t)
                rest(0, rows, at, [part[v, 8 * t : 8 * t + 8, :] for v in range(V)])
            for t in (-1, 4):
                rows, at = tile(t)
                rest(0, rows, at, [of_k(0, v, rows, at) for v in range(V)])
            for t in range(4):
                rows, at = tile(t)
                rest(1, rows, at, [of_k(1, v, rows, at) for v in range(V)])

        @pl.when(is_near)
        def _():
            before(near_k, near_rest)

        @pl.when(jnp.logical_not(is_near))
        def _():
            before(off_k, off_rest)

        @pl.when(has_low)
        def _():
            up.wait_recv()
            for v in range(V):
                u[0, v, TOP - 6 : TOP, :] = up_in[it, 6 * v : 6 * v + 6, :]
            if opening:
                frozen[5:8, :] = up_in[it, 30:33, :]
                const_up.wait_recv()
                for n, (ref, at) in enumerate(constants):
                    ref[at + (slice(5, 8), slice(None))] = const_up_in[3 * n : 3 * n + 3, :]

        @pl.when(has_high)
        def _():
            down.wait_recv()
            for v in range(V):
                u[0, v, TOP + NJ : TOP + NJ + 4, :] = down_in[it, 4 * v : 4 * v + 4, :]
            if opening:
                frozen[8 + NJ : 10 + NJ, :] = down_in[it, 20:22, :]
                const_down.wait_recv()
                for n, (ref, at) in enumerate(constants):
                    ref[at + (slice(8 + NJ, 10 + NJ), slice(None))] = const_down_in[2 * n : 2 * n + 2, :]

        @pl.when(is_near)
        def _():
            after(near_k, near_rest)

        @pl.when(jnp.logical_not(is_near))
        def _():
            after(off_k, off_rest)

        @pl.when(has_low)
        def _():
            down.wait_send()
            if opening:
                const_down.wait_send()

        @pl.when(has_high)
        def _():
            up.wait_send()
            if opening:
                const_up.wait_send()

    sweep(0, True)

    def later(it, c):
        sweep(it, False)
        return c

    lax.fori_loop(1, ITERS, later, 0)

    for v in range(V):
        out[v] = u[0, v, TOP : TOP + NJ, :]


def on_device(field, source, block_inverse, coupling, donor_base, donor_weight, receiver_cell):
    blocks = donor_base.shape[2]
    hbm = pl.BlockSpec(memory_space=pl.ANY)
    result = pl.pallas_call(
        functools.partial(kernel, blocks),
        out_shape=jax.ShapeDtypeStruct((V, NJ, NK), f32),
        in_specs=[hbm] * 7,
        out_specs=pl.BlockSpec(memory_space=pltpu.VMEM),
        scratch_shapes=[
            pltpu.VMEM((V, NJ + 16, NK), f32),
            pltpu.VMEM((V, V, NJ + 16, NK), f32),
            pltpu.VMEM((4, NJ + 16, NK), f32),
            pltpu.VMEM((blocks, S), i32),
            pltpu.VMEM((4, blocks, S), f32),
            pltpu.VMEM((blocks, S), i32),
            pltpu.VMEM((2, V, 2 * TOP + NJ, NK), f32),
            pltpu.VMEM((480, NK // 2), bf16),
            pltpu.VMEM((480, NK // 2), f8),
            pltpu.VMEM((NK, NK), bf16),
            pltpu.VMEM((NK, NK), bf16),
            pltpu.VMEM((blocks, NK // 2, S), bf16),
            pltpu.VMEM((blocks, NK // 2, S), f8),
            pltpu.VMEM((blocks, 3, NJ, S), f32),
            pltpu.VMEM((blocks * S, NK // 2), bf16),
            pltpu.VMEM((blocks * S, NK // 2), f8),
            pltpu.VMEM((blocks, 8, S), f32),
            pltpu.VMEM((ITERS, blocks, 8, S), f32),
            pltpu.VMEM((2, 160, NK // 2), f32),
            pltpu.VMEM((32, NK // 2), f32),
            pltpu.VMEM((NJ + 16, NK), f32),
            pltpu.VMEM((V, NJ, NK), f32),
            pltpu.VMEM((24, NK), f32),
            pltpu.VMEM((40, NK), f32),
            pltpu.VMEM((ITERS, 24, NK), f32),
            pltpu.VMEM((ITERS, 40, NK), f32),
            pltpu.VMEM((72, NK), f32),
            pltpu.VMEM((104, NK), f32),
            pltpu.VMEM((72, NK), f32),
            pltpu.VMEM((104, NK), f32),
            pltpu.SemaphoreType.DMA,
            pltpu.SemaphoreType.DMA((ITERS, blocks // G)),
            pltpu.SemaphoreType.DMA((4,)),
            pltpu.SemaphoreType.DMA((ITERS, 4)),
            pltpu.SemaphoreType.DMA((7,)),
        ],
        compiler_params=pltpu.CompilerParams(
            collective_id=0, has_side_effects=True, vmem_limit_bytes=63 * 2**20
        ),
    )(
        field[0, 0],
        source[0, 0],
        block_inverse[0, 0],
        coupling[0, 0],
        donor_base[0, 0],
        donor_weight[0, 0],
        receiver_cell[0, 0],
    )
    return result[None, None]


def solution(mesh):
    in_specs = (
        P("group", "blk", None, None, None),
        P("group", "blk", None, None, None),
        P("group", "blk", None, None, None, None),
        P("group", "blk", None, None, None),
        P("group", "blk", None, None),
        P("group", "blk", None, None, None),
        P("group", "blk", None, None),
    )
    out_specs = P("group", "blk", None, None, None)
    return jax.shard_map(
        on_device, mesh=mesh, in_specs=in_specs, out_specs=out_specs, check_vma=False
    )
```

```python
import functools

import jax
import jax.numpy as jnp
from jax import lax
from jax.experimental import pallas as pl
from jax.experimental.pallas import tpu as pltpu
from jax.sharding import PartitionSpec as P

ITERS = 4
V = 5
NJ = 32
NK = 512
S = 256
TOP = 16
G = 8

upwind_offsets = (-3, -2, -1, 0, 1, 2)
upwind_weights = (-2.0 / 60.0, 15.0 / 60.0, -60.0 / 60.0, 20.0 / 60.0, 30.0 / 60.0, -3.0 / 60.0)

f32, bf16, i32 = jnp.float32, jnp.bfloat16, jnp.int32
f8 = jnp.float8_e4m3fn
LIFT = 65536.0
MESH = pl.DeviceIdType.MESH


def shift_k(x, o):
    if o == 0:
        return x
    n = x.shape[1]
    col = lax.broadcasted_iota(i32, x.shape, 1)
    rolled = pltpu.roll(x, (-o) % n, axis=1)
    keep = (col + o >= 0) & (col + o < n)
    return jnp.where(keep, rolled, 0.0)


def split(x):
    hi = x.astype(bf16)
    return hi, (x - hi.astype(f32)).astype(bf16)


def largest(x):
    m = jnp.max(jnp.max(jnp.abs(x), axis=1, keepdims=True), axis=0, keepdims=True)
    return jnp.maximum(m, 1e-30)


def swap_columns(inverse):
    a = lax.broadcasted_iota(i32, (NK, NK), 1 if inverse else 0)
    c = lax.broadcasted_iota(i32, (NK, NK), 0 if inverse else 1)
    return jnp.where(a == 2 * (c & (NK // 2 - 1)) + (c >> 8), 1.0, 0.0).astype(bf16)


def make_table(u, tab, tab8, pick):
    a = jnp.concatenate([u[0, v, TOP : TOP + NJ, :] for v in range(V)], axis=0)
    m = largest(a)
    t = jnp.dot(
        jnp.concatenate(split(a * (LIFT / m)), axis=0), pick[...], preferred_element_type=f32
    )
    t0, t1 = t[:, : NK // 2], t[:, NK // 2 :]
    first = jnp.concatenate([t0[1:, :1], jnp.zeros((1, 1), f32)], axis=0)
    t2 = jnp.concatenate([t0[:, 1:], first], axis=1)
    for o, p in enumerate((t0, t1, t2)):
        tab[pl.ds(160 * o, 160), :] = p[:160].astype(bf16)
        tab8[pl.ds(160 * o, 160), :] = p[160:].astype(f8)
    return m * (1.0 / LIFT)


def one_hot(base):
    k = (base & (NK - 1)) >> 1
    return jnp.where(lax.broadcasted_iota(i32, (NK // 2, S), 0) == k, 1.0, 0.0)


def patterns(base, w):
    even = (base & 1) == 0
    row = lax.broadcasted_iota(i32, (NJ, S), 0)
    here, below = row == (base >> 9), row == (base >> 9) + 1
    zero = jnp.zeros_like(w[0])

    def spread(x, y):
        return jnp.where(here, x, jnp.where(below, y, 0.0))

    return (
        spread(jnp.where(even, w[0], zero), jnp.where(even, w[2], zero)),
        spread(jnp.where(even, w[1], w[0]), jnp.where(even, w[3], w[2])),
        spread(jnp.where(even, zero, w[1]), jnp.where(even, zero, w[3])),
    )


def interpolate(tab, tab8, hot, hot8, ps, undo):
    high = jnp.dot(tab[...], hot, preferred_element_type=f32)
    low = jnp.dot(tab8[...], hot8, preferred_element_type=f32)
    rows = []
    for v in range(V):
        total = None
        for o in range(3):
            at = 160 * o + 32 * v
            term = (high[at : at + 32] + low[at : at + 32]) * ps[o]
            total = term if total is None else total + term
        rows.append(jnp.sum(total, axis=0, keepdims=True))
    return jnp.concatenate(rows + [jnp.zeros((3, S), f32)], axis=0) * undo


def rows_of(half):
    r = lax.broadcasted_iota(i32, (16, S), 0)
    return r + 8 if half else jnp.where(r < 8, r, r + 16)


def kernel(
    blocks,
    field_hbm, source_hbm, inverse_hbm, coupling_hbm, base_hbm, weight_hbm, cell_hbm,
    out,
    source, inverse, coupling, base, weight, cell,
    u, tab, tab8, pick, spread, hots, hots8, pats, cell_hots, cell_hots8,
    send, recv, acc, marks, frozen, part,
    down_out, up_out, down_in, up_in, const_down_out, const_up_out, const_down_in, const_up_in,
    send_sem, recv_sem, hsend_sem, hrecv_sem, in_sem,
):
    g = lax.axis_index("group")
    b = lax.axis_index("blk")
    groups = blocks // G
    other = 1 - g
    is_near = g == 0
    has_low, has_high = b > 0, b < blocks - 1

    def block_rows(ref):
        return ref.at[0, :, pl.ds(TOP, NJ), :]

    loads = [
        pltpu.make_async_copy(a, c, in_sem.at[n])
        for n, (a, c) in enumerate(
            (
                (field_hbm, block_rows(u)),
                (base_hbm, base),
                (weight_hbm, weight),
                (cell_hbm, cell),
                (source_hbm, source.at[:, pl.ds(8, NJ), :]),
                (coupling_hbm, coupling.at[:, pl.ds(8, NJ), :]),
                (inverse_hbm, inverse.at[:, :, pl.ds(8, NJ), :]),
            )
        )
    ]
    for load in loads:
        load.start()

    barrier = pltpu.get_barrier_semaphore()

    def greet(d, c):
        pl.semaphore_signal(barrier, inc=1, device_id=(other, d), device_id_type=MESH)
        return c

    lax.fori_loop(0, blocks, greet, 0)

    for d in ((b + blocks - 1) % blocks, (b + 1) % blocks):
        pl.semaphore_signal(barrier, inc=1, device_id=(g, d), device_id_type=MESH)

    edge_tiles = (slice(0, 8), slice(8 + NJ, 16 + NJ))
    for v in range(V):
        u[0, v, 0:TOP, :] = jnp.zeros((TOP, NK), f32)
        u[0, v, TOP + NJ : 2 * TOP + NJ, :] = jnp.zeros((TOP, NK), f32)
    constants = (
        [(source, (v,)) for v in range(V)]
        + [(inverse, (v, w)) for v in range(V) for w in range(V)]
        + [(coupling, (n,)) for n in range(4)]
    )
    for ref, at in constants + [(frozen, ())]:
        for rows in edge_tiles:
            ref[at + (rows, slice(None))] = jnp.zeros((8, NK), f32)
    for ref in (down_out, up_out, const_down_out, const_up_out):
        ref[...] = jnp.zeros_like(ref)

    pick[...] = swap_columns(False)
    spread[...] = swap_columns(True)

    for load in loads[:3]:
        load.wait()

    def far_first(n):
        return 2 + ((n + 1) // 2) * (1 - 2 * (n % 2))

    def partner(turn, q, sign):
        dz, dy, dx = far_first(turn // 2), far_first(2 * (turn % 2) + q // 4), far_first(q % 4)
        z, y, x = b // 16, (b // 4) % 4, b % 4
        return (
            ((z + 4 + sign * dz) % 4) * 16
            + ((y + 4 + sign * dy) % 4) * 4
            + (x + 4 + sign * dx) % 4
        )

    def message(it, turn, q):
        return pltpu.make_async_remote_copy(
            src_ref=send.at[turn * G + q],
            dst_ref=recv.at[it, turn * G + q],
            send_sem=send_sem,
            recv_sem=recv_sem.at[it, turn],
            device_id=(other, partner(turn, q, 1)),
            device_id_type=MESH,
        )

    def ship(src, dst, n, direction, slot):
        return pltpu.make_async_remote_copy(
            src_ref=src,
            dst_ref=dst,
            send_sem=hsend_sem.at[n],
            recv_sem=hrecv_sem.at[slot, n],
            device_id=(g, b + direction),
            device_id_type=MESH,
        )

    def edges(it, rows):
        return (
            ship(down_out, down_in.at[it], 0, -1, it),
            ship(up_out.at[pl.ds(0, rows)], up_in.at[it, pl.ds(0, rows)], 1, 1, it),
        )

    def const_edges():
        return (
            ship(const_down_out, const_down_in, 2, -1, 0),
            ship(const_up_out, const_up_in, 3, 1, 0),
        )

    def sweep(it, opening):
        undo = make_table(u, tab, tab8, pick)

        def gather_group(turn, c):
            first = pl.multiple_of(turn * G, G)
            for q in range(G):
                if opening:
                    d = partner(turn, q, 1)
                    at = base[pl.ds(d, 1), :]
                    hot = one_hot(at)
                    hot, hot8 = hot.astype(bf16), hot.astype(f8)
                    ps = patterns(at, [weight[n, pl.ds(d, 1), :] for n in range(4)])
                    hots[first + q] = hot
                    hots8[first + q] = hot8
                    for o in range(3):
                        pats[first + q, o] = ps[o]
                else:
                    hot, hot8 = hots[first + q], hots8[first + q]
                    ps = [pats[first + q, o] for o in range(3)]
                send[first + q] = interpolate(tab, tab8, hot, hot8, ps, undo)
                if q == 3:
                    if opening:

                        @pl.when(turn == 0)
                        def _():
                            pl.semaphore_wait(barrier, blocks + 2)

                    for n in range(4):
                        message(it, turn, n).start()
            for n in range(4, G):
                message(it, turn, n).start()
            return c

        lax.fori_loop(0, groups, gather_group, 0)

        if opening:
            for load in loads[3:]:
                load.wait()
            for n, (ref, at) in enumerate(constants):
                const_down_out[2 * n : 2 * n + 2, :] = ref[at + (slice(8, 10), slice(None))]
                const_up_out[3 * n : 3 * n + 3, :] = ref[at + (slice(5 + NJ, 8 + NJ), slice(None))]
            const_down, const_up = const_edges()

            @pl.when(has_low)
            def _():
                const_down.start()

            @pl.when(has_high)
            def _():
                const_up.start()


        def scatter_group(turn, c, half):
            first = pl.multiple_of(turn * G, G)
            if not half:
                pltpu.make_async_copy(
                    recv.at[it, pl.ds(first, G)],
                    recv.at[it, pl.ds(first, G)],
                    recv_sem.at[it, turn],
                ).wait()
            cells = jnp.concatenate(
                [cell[pl.ds(partner(turn, q, -1), 1), :] for q in range(G)], axis=0
            )
            slots = pl.ds(pl.multiple_of(first * S, S), G * S)
            if opening and not half:
                down_cells = jnp.transpose(cells.astype(f32)).astype(i32)
                for q in range(G):
                    hot = jnp.where(
                        lax.broadcasted_iota(i32, (S, NK // 2), 1)
                        == (down_cells[:, q : q + 1] & (NK - 1)) >> 1,
                        1.0,
                        0.0,
                    )
                    at = pl.ds(pl.multiple_of((first + q) * S, S), S)
                    cell_hots[at, :] = hot.astype(bf16)
                    cell_hots8[at, :] = hot.astype(f8)
            vals = [recv[it, first + q] for q in range(G)]
            m = largest(functools.reduce(jnp.maximum, [jnp.abs(x) for x in vals]))
            scale = LIFT / m
            highs, lows = [], []
            for q in range(G):
                r = cells[q : q + 1]
                hit = rows_of(half) == (r >> 9)
                even = (r & 1) == 0
                hits = (hit & even, hit & jnp.logical_not(even))
                high = vals[q].astype(bf16).astype(f32)
                low = (vals[q] - high) * scale
                rows = [jnp.where(x, high[v : v + 1], 0.0) for x in hits for v in range(V)]
                if opening:
                    rows += [jnp.where(x, 1.0, 0.0) for x in hits]
                highs.append(jnp.concatenate(rows, axis=0).astype(bf16))
                rows = [jnp.where(x, low[v : v + 1], 0.0) for x in hits for v in range(V)]
                lows.append(jnp.concatenate(rows, axis=0).astype(f8))
            p = jnp.dot(
                jnp.concatenate(highs, axis=1), cell_hots[slots, :], preferred_element_type=f32
            )
            acc[0] += p[:160]
            if opening:
                marks[...] += p[160:]
            p = jnp.dot(
                jnp.concatenate(lows, axis=1), cell_hots8[slots, :], preferred_element_type=f32
            )
            acc[1] += p * (m * (1.0 / LIFT))
            return c

        def interleave(even, odd):
            pair = jnp.concatenate([even, odd], axis=1).astype(bf16)
            return jnp.dot(pair, spread[...], preferred_element_type=f32)

        def place(half):
            acc[...] = jnp.zeros_like(acc)
            if opening:
                marks[...] = jnp.zeros_like(marks)
            lax.fori_loop(0, groups, functools.partial(scatter_group, half=half), 0)
            placed = interleave(acc[0, :80, :], acc[0, 80:, :]) + interleave(acc[1, :80, :], acc[1, 80:, :])
            pieces = ((0, 8), (8, 16)) if half else ((0, 0), (8, 24))
            if opening:
                mark = interleave(marks[:16, :], marks[16:, :])
            for n, j in pieces:
                if opening:
                    frozen[8 + j : 16 + j, :] = mark[n : n + 8]
                fixed = frozen[8 + j : 16 + j, :] > 0.5
                for v in range(V):
                    at = TOP + j
                    u[0, v, at : at + 8, :] = jnp.where(
                        fixed, placed[16 * v + n : 16 * v + n + 8], u[0, v, at : at + 8, :]
                    )

        place(0)

        for v in range(V):
            down_out[4 * v : 4 * v + 4, :] = u[0, v, TOP : TOP + 4, :]
            up_out[6 * v : 6 * v + 6, :] = u[0, v, TOP + NJ - 6 : TOP + NJ, :]
        if opening:
            down_out[20:22, :] = frozen[8:10, :]
            up_out[30:33, :] = frozen[5 + NJ : 8 + NJ, :]
        down, up = edges(it, 40 if opening else 32)

        @pl.when(has_low)
        def _():
            down.start()

        @pl.when(has_high)
        def _():
            up.start()

        place(1)

        pltpu.make_async_copy(send, send, send_sem).wait()

        def apply(rows, ts, v):
            return sum(inverse[v, w, rows, :] * ts[w] for w in range(V))

        def near_k(h, v, rows, at):
            x = u[h, v, at : at + 8, :]
            return (
                source[v, rows, :]
                + coupling[2, rows, :] * shift_k(x, -1)
                + coupling[3, rows, :] * shift_k(x, 1)
            )

        def near_rest(h, rows, at, along_k):
            ts = [
                along_k[v]
                + coupling[0, rows, :] * u[h, v, at - 1 : at + 7, :]
                + coupling[1, rows, :] * u[h, v, at + 1 : at + 9, :]
                for v in range(V)
            ]
            parity = (
                lax.broadcasted_iota(i32, (8, NK), 0) + lax.broadcasted_iota(i32, (8, NK), 1)
            ) & 1
            update = (frozen[rows, :] < 0.5) & (parity == h)
            for v in range(V):
                u[1 - h, v, at : at + 8, :] = jnp.where(
                    update, apply(rows, ts, v), u[h, v, at : at + 8, :]
                )

        def off_k(h, v, rows, at):
            x = u[h, v, at : at + 8, :]
            along = sum(a * shift_k(x, o) for o, a in zip(upwind_offsets, upwind_weights))
            return source[v, rows, :] - coupling[1, rows, :] * along

        def off_rest(h, rows, at, along_k):
            ts = []
            for v in range(V):
                along = sum(
                    a * u[h, v, at + o : at + o + 8, :]
                    for o, a in zip(upwind_offsets, upwind_weights)
                )
                ts.append(along_k[v] - coupling[0, rows, :] * along)
            update = frozen[rows, :] < 0.5
            for v in range(V):
                old = u[h, v, at : at + 8, :]
                u[1 - h, v, at : at + 8, :] = jnp.where(update, old + apply(rows, ts, v), old)

        def tile(t):
            return slice(8 * t + 8, 8 * t + 16), TOP + 8 * t

        def before(of_k, rest):
            for t in range(4):
                rows, at = tile(t)
                along_k = [of_k(0, v, rows, at) for v in range(V)]
                if t in (1, 2):
                    rest(0, rows, at, along_k)
                else:
                    for v in range(V):
                        part[v, 8 * t : 8 * t + 8, :] = along_k[v]

        def after(of_k, rest):
            for t in (0, 3):
                rows, at = tile(t)
                rest(0, rows, at, [part[v, 8 * t : 8 * t + 8, :] for v in range(V)])
            for t in (-1, 4):
                rows, at = tile(t)
                rest(0, rows, at, [of_k(0, v, rows, at) for v in range(V)])
            for t in range(4):
                rows, at = tile(t)
                rest(1, rows, at, [of_k(1, v, rows, at) for v in range(V)])

        @pl.when(is_near)
        def _():
            before(near_k, near_rest)

        @pl.when(jnp.logical_not(is_near))
        def _():
            before(off_k, off_rest)

        @pl.when(has_low)
        def _():
            up.wait_recv()
            for v in range(V):
                u[0, v, TOP - 6 : TOP, :] = up_in[it, 6 * v : 6 * v + 6, :]
            if opening:
                frozen[5:8, :] = up_in[it, 30:33, :]
                const_up.wait_recv()
                for n, (ref, at) in enumerate(constants):
                    ref[at + (slice(5, 8), slice(None))] = const_up_in[3 * n : 3 * n + 3, :]

        @pl.when(has_high)
        def _():
            down.wait_recv()
            for v in range(V):
                u[0, v, TOP + NJ : TOP + NJ + 4, :] = down_in[it, 4 * v : 4 * v + 4, :]
            if opening:
                frozen[8 + NJ : 10 + NJ, :] = down_in[it, 20:22, :]
                const_down.wait_recv()
                for n, (ref, at) in enumerate(constants):
                    ref[at + (slice(8 + NJ, 10 + NJ), slice(None))] = const_down_in[2 * n : 2 * n + 2, :]

        @pl.when(is_near)
        def _():
            after(near_k, near_rest)

        @pl.when(jnp.logical_not(is_near))
        def _():
            after(off_k, off_rest)

        @pl.when(has_low)
        def _():
            down.wait_send()
            if opening:
                const_down.wait_send()

        @pl.when(has_high)
        def _():
            up.wait_send()
            if opening:
                const_up.wait_send()

    sweep(0, True)

    def later(it, c):
        sweep(it, False)
        return c

    lax.fori_loop(1, ITERS, later, 0)

    for v in range(V):
        out[v] = u[0, v, TOP : TOP + NJ, :]


def on_device(field, source, block_inverse, coupling, donor_base, donor_weight, receiver_cell):
    blocks = donor_base.shape[2]
    hbm = pl.BlockSpec(memory_space=pl.ANY)
    result = pl.pallas_call(
        functools.partial(kernel, blocks),
        out_shape=jax.ShapeDtypeStruct((V, NJ, NK), f32),
        in_specs=[hbm] * 7,
        out_specs=pl.BlockSpec(memory_space=pltpu.VMEM),
        scratch_shapes=[
            pltpu.VMEM((V, NJ + 16, NK), f32),
            pltpu.VMEM((V, V, NJ + 16, NK), f32),
            pltpu.VMEM((4, NJ + 16, NK), f32),
            pltpu.VMEM((blocks, S), i32),
            pltpu.VMEM((4, blocks, S), f32),
            pltpu.VMEM((blocks, S), i32),
            pltpu.VMEM((2, V, 2 * TOP + NJ, NK), f32),
            pltpu.VMEM((480, NK // 2), bf16),
            pltpu.VMEM((480, NK // 2), f8),
            pltpu.VMEM((NK, NK), bf16),
            pltpu.VMEM((NK, NK), bf16),
            pltpu.VMEM((blocks, NK // 2, S), bf16),
            pltpu.VMEM((blocks, NK // 2, S), f8),
            pltpu.VMEM((blocks, 3, NJ, S), f32),
            pltpu.VMEM((blocks * S, NK // 2), bf16),
            pltpu.VMEM((blocks * S, NK // 2), f8),
            pltpu.VMEM((blocks, 8, S), f32),
            pltpu.VMEM((ITERS, blocks, 8, S), f32),
            pltpu.VMEM((2, 160, NK // 2), f32),
            pltpu.VMEM((32, NK // 2), f32),
            pltpu.VMEM((NJ + 16, NK), f32),
            pltpu.VMEM((V, NJ, NK), f32),
            pltpu.VMEM((24, NK), f32),
            pltpu.VMEM((40, NK), f32),
            pltpu.VMEM((ITERS, 24, NK), f32),
            pltpu.VMEM((ITERS, 40, NK), f32),
            pltpu.VMEM((72, NK), f32),
            pltpu.VMEM((104, NK), f32),
            pltpu.VMEM((72, NK), f32),
            pltpu.VMEM((104, NK), f32),
            pltpu.SemaphoreType.DMA,
            pltpu.SemaphoreType.DMA((ITERS, blocks // G)),
            pltpu.SemaphoreType.DMA((4,)),
            pltpu.SemaphoreType.DMA((ITERS, 4)),
            pltpu.SemaphoreType.DMA((7,)),
        ],
        compiler_params=pltpu.CompilerParams(
            collective_id=0, has_side_effects=True, vmem_limit_bytes=63 * 2**20
        ),
    )(
        field[0, 0],
        source[0, 0],
        block_inverse[0, 0],
        coupling[0, 0],
        donor_base[0, 0],
        donor_weight[0, 0],
        receiver_cell[0, 0],
    )
    return result[None, None]


def solution(mesh):
    in_specs = (
        P("group", "blk", None, None, None),
        P("group", "blk", None, None, None),
        P("group", "blk", None, None, None, None),
        P("group", "blk", None, None, None),
        P("group", "blk", None, None),
        P("group", "blk", None, None, None),
        P("group", "blk", None, None),
    )
    out_specs = P("group", "blk", None, None, None)
    return jax.shard_map(
        on_device, mesh=mesh, in_specs=in_specs, out_specs=out_specs, check_vma=False
    )
```

```python
import functools

import jax
import jax.numpy as jnp
from jax import lax
from jax.experimental import pallas as pl
from jax.experimental.pallas import tpu as pltpu
from jax.sharding import PartitionSpec as P

ITERS = 4
V = 5
NJ = 32
NK = 512
S = 256
TOP = 16
G = 8

upwind_offsets = (-3, -2, -1, 0, 1, 2)
upwind_weights = (-2.0 / 60.0, 15.0 / 60.0, -60.0 / 60.0, 20.0 / 60.0, 30.0 / 60.0, -3.0 / 60.0)

f32, bf16, i32 = jnp.float32, jnp.bfloat16, jnp.int32
f8 = jnp.float8_e4m3fn
LIFT = 65536.0
MESH = pl.DeviceIdType.MESH


def shift_k(x, o):
    if o == 0:
        return x
    n = x.shape[1]
    col = lax.broadcasted_iota(i32, x.shape, 1)
    rolled = pltpu.roll(x, (-o) % n, axis=1)
    keep = (col + o >= 0) & (col + o < n)
    return jnp.where(keep, rolled, 0.0)


def split(x):
    hi = x.astype(bf16)
    return hi, (x - hi.astype(f32)).astype(bf16)


def largest(x):
    m = jnp.max(jnp.max(jnp.abs(x), axis=1, keepdims=True), axis=0, keepdims=True)
    return jnp.maximum(m, 1e-30)


def swap_columns(inverse):
    a = lax.broadcasted_iota(i32, (NK, NK), 1 if inverse else 0)
    c = lax.broadcasted_iota(i32, (NK, NK), 0 if inverse else 1)
    return jnp.where(a == 2 * (c & (NK // 2 - 1)) + (c >> 8), 1.0, 0.0).astype(bf16)


def make_table(u, tab, tab8, pick):
    a = jnp.concatenate([u[0, v, TOP : TOP + NJ, :] for v in range(V)], axis=0)
    m = largest(a)
    t = jnp.dot(
        jnp.concatenate(split(a * (LIFT / m)), axis=0), pick[...], preferred_element_type=f32
    )
    t0, t1 = t[:, : NK // 2], t[:, NK // 2 :]
    first = jnp.concatenate([t0[1:, :1], jnp.zeros((1, 1), f32)], axis=0)
    t2 = jnp.concatenate([t0[:, 1:], first], axis=1)
    for o, p in enumerate((t0, t1, t2)):
        tab[pl.ds(160 * o, 160), :] = p[:160].astype(bf16)
        tab8[pl.ds(160 * o, 160), :] = p[160:].astype(f8)
    return m * (1.0 / LIFT)


def one_hot(base):
    k = (base & (NK - 1)) >> 1
    return jnp.where(lax.broadcasted_iota(i32, (NK // 2, S), 0) == k, 1.0, 0.0)


def patterns(base, w):
    even = (base & 1) == 0
    row = lax.broadcasted_iota(i32, (NJ, S), 0)
    here, below = row == (base >> 9), row == (base >> 9) + 1
    zero = jnp.zeros_like(w[0])

    def spread(x, y):
        return jnp.where(here, x, jnp.where(below, y, 0.0))

    return (
        spread(jnp.where(even, w[0], zero), jnp.where(even, w[2], zero)),
        spread(jnp.where(even, w[1], w[0]), jnp.where(even, w[3], w[2])),
        spread(jnp.where(even, zero, w[1]), jnp.where(even, zero, w[3])),
    )


def interpolate(tab, tab8, hot, hot8, ps, undo):
    high = jnp.dot(tab[...], hot, preferred_element_type=f32)
    low = jnp.dot(tab8[...], hot8, preferred_element_type=f32)
    rows = []
    for v in range(V):
        total = None
        for o in range(3):
            at = 160 * o + 32 * v
            term = (high[at : at + 32] + low[at : at + 32]) * ps[o]
            total = term if total is None else total + term
        rows.append(jnp.sum(total, axis=0, keepdims=True))
    return jnp.concatenate(rows + [jnp.zeros((3, S), f32)], axis=0) * undo


def rows_of(half):
    r = lax.broadcasted_iota(i32, (16, S), 0)
    return r + 8 if half else jnp.where(r < 8, r, r + 16)


def kernel(
    blocks,
    field_hbm, source_hbm, inverse_hbm, coupling_hbm, base_hbm, weight_hbm, cell_hbm,
    out,
    source, inverse, coupling, base, weight, cell,
    u, tab, tab8, pick, spread, hots, hots8, pats, cell_hots, cell_hots8,
    send, recv, acc, marks, frozen, part,
    down_out, up_out, down_in, up_in, const_down_out, const_up_out, const_down_in, const_up_in,
    send_sem, recv_sem, hsend_sem, hrecv_sem, in_sem,
):
    g = lax.axis_index("group")
    b = lax.axis_index("blk")
    groups = blocks // G
    other = 1 - g
    is_near = g == 0
    has_low, has_high = b > 0, b < blocks - 1

    def block_rows(ref):
        return ref.at[0, :, pl.ds(TOP, NJ), :]

    loads = [
        pltpu.make_async_copy(a, c, in_sem.at[n])
        for n, (a, c) in enumerate(
            (
                (field_hbm, block_rows(u)),
                (base_hbm, base),
                (weight_hbm, weight),
                (cell_hbm, cell),
                (source_hbm, source.at[:, pl.ds(8, NJ), :]),
                (coupling_hbm, coupling.at[:, pl.ds(8, NJ), :]),
                (inverse_hbm, inverse.at[:, :, pl.ds(8, NJ), :]),
            )
        )
    ]
    for load in loads:
        load.start()

    barrier = pltpu.get_barrier_semaphore()

    def greet(d, c):
        pl.semaphore_signal(barrier, inc=1, device_id=(other, d), device_id_type=MESH)
        return c

    lax.fori_loop(0, blocks, greet, 0)

    for d in ((b + blocks - 1) % blocks, (b + 1) % blocks):
        pl.semaphore_signal(barrier, inc=1, device_id=(g, d), device_id_type=MESH)

    edge_tiles = (slice(0, 8), slice(8 + NJ, 16 + NJ))
    for v in range(V):
        u[0, v, 0:TOP, :] = jnp.zeros((TOP, NK), f32)
        u[0, v, TOP + NJ : 2 * TOP + NJ, :] = jnp.zeros((TOP, NK), f32)
    constants = (
        [(source, (v,)) for v in range(V)]
        + [(inverse, (v, w)) for v in range(V) for w in range(V)]
        + [(coupling, (n,)) for n in range(4)]
    )
    for ref, at in constants + [(frozen, ())]:
        for rows in edge_tiles:
            ref[at + (rows, slice(None))] = jnp.zeros((8, NK), f32)
    for ref in (down_out, up_out, const_down_out, const_up_out):
        ref[...] = jnp.zeros_like(ref)

    pick[...] = swap_columns(False)
    spread[...] = swap_columns(True)

    for load in loads[:3]:
        load.wait()

    def far_first(n):
        return 2 + ((n + 1) // 2) * (1 - 2 * (n % 2))

    def partner(turn, q, sign):
        dz, dy, dx = far_first(turn // 2), far_first(2 * (turn % 2) + q // 4), far_first(q % 4)
        z, y, x = b // 16, (b // 4) % 4, b % 4
        return (
            ((z + 4 + sign * dz) % 4) * 16
            + ((y + 4 + sign * dy) % 4) * 4
            + (x + 4 + sign * dx) % 4
        )

    def message(it, turn, q):
        return pltpu.make_async_remote_copy(
            src_ref=send.at[turn * G + q],
            dst_ref=recv.at[it, turn * G + q],
            send_sem=send_sem,
            recv_sem=recv_sem.at[it, turn],
            device_id=(other, partner(turn, q, 1)),
            device_id_type=MESH,
        )

    def ship(src, dst, n, direction, slot):
        return pltpu.make_async_remote_copy(
            src_ref=src,
            dst_ref=dst,
            send_sem=hsend_sem.at[n],
            recv_sem=hrecv_sem.at[slot, n],
            device_id=(g, b + direction),
            device_id_type=MESH,
        )

    def edges(it, rows):
        return (
            ship(down_out, down_in.at[it], 0, -1, it),
            ship(up_out.at[pl.ds(0, rows)], up_in.at[it, pl.ds(0, rows)], 1, 1, it),
        )

    def const_edges():
        return (
            ship(const_down_out, const_down_in, 2, -1, 0),
            ship(const_up_out, const_up_in, 3, 1, 0),
        )

    def sweep(it, opening):
        undo = make_table(u, tab, tab8, pick)

        def gather_group(turn, c):
            first = pl.multiple_of(turn * G, G)
            for q in range(G):
                if opening:
                    d = partner(turn, q, 1)
                    at = base[pl.ds(d, 1), :]
                    hot = one_hot(at)
                    hot, hot8 = hot.astype(bf16), hot.astype(f8)
                    ps = patterns(at, [weight[n, pl.ds(d, 1), :] for n in range(4)])
                    hots[first + q] = hot
                    hots8[first + q] = hot8
                    for o in range(3):
                        pats[first + q, o] = ps[o]
                else:
                    hot, hot8 = hots[first + q], hots8[first + q]
                    ps = [pats[first + q, o] for o in range(3)]
                send[first + q] = interpolate(tab, tab8, hot, hot8, ps, undo)
            if opening:

                @pl.when(turn == 0)
                def _():
                    pl.semaphore_wait(barrier, blocks + 2)

            for n in range(G):
                message(it, turn, n).start()
            return c

        lax.fori_loop(0, groups, gather_group, 0)

        if opening:
            for load in loads[3:]:
                load.wait()
            for n, (ref, at) in enumerate(constants):
                const_down_out[2 * n : 2 * n + 2, :] = ref[at + (slice(8, 10), slice(None))]
                const_up_out[3 * n : 3 * n + 3, :] = ref[at + (slice(5 + NJ, 8 + NJ), slice(None))]
            const_down, const_up = const_edges()

            @pl.when(has_low)
            def _():
                const_down.start()

            @pl.when(has_high)
            def _():
                const_up.start()


        def scatter_group(turn, c, half):
            first = pl.multiple_of(turn * G, G)
            if not half:
                pltpu.make_async_copy(
                    recv.at[it, pl.ds(first, G)],
                    recv.at[it, pl.ds(first, G)],
                    recv_sem.at[it, turn],
                ).wait()
            cells = jnp.concatenate(
                [cell[pl.ds(partner(turn, q, -1), 1), :] for q in range(G)], axis=0
            )
            slots = pl.ds(pl.multiple_of(first * S, S), G * S)
            if opening and not half:
                down_cells = jnp.transpose(cells.astype(f32)).astype(i32)
                for q in range(G):
                    hot = jnp.where(
                        lax.broadcasted_iota(i32, (S, NK // 2), 1)
                        == (down_cells[:, q : q + 1] & (NK - 1)) >> 1,
                        1.0,
                        0.0,
                    )
                    at = pl.ds(pl.multiple_of((first + q) * S, S), S)
                    cell_hots[at, :] = hot.astype(bf16)
                    cell_hots8[at, :] = hot.astype(f8)
            vals = [recv[it, first + q] for q in range(G)]
            m = largest(functools.reduce(jnp.maximum, [jnp.abs(x) for x in vals]))
            scale = LIFT / m
            highs, lows = [], []
            for q in range(G):
                r = cells[q : q + 1]
                hit = rows_of(half) == (r >> 9)
                even = (r & 1) == 0
                hits = (hit & even, hit & jnp.logical_not(even))
                high = vals[q].astype(bf16).astype(f32)
                low = (vals[q] - high) * scale
                rows = [jnp.where(x, high[v : v + 1], 0.0) for x in hits for v in range(V)]
                if opening:
                    rows += [jnp.where(x, 1.0, 0.0) for x in hits]
                highs.append(jnp.concatenate(rows, axis=0).astype(bf16))
                rows = [jnp.where(x, low[v : v + 1], 0.0) for x in hits for v in range(V)]
                lows.append(jnp.concatenate(rows, axis=0).astype(f8))
            p = jnp.dot(
                jnp.concatenate(highs, axis=1), cell_hots[slots, :], preferred_element_type=f32
            )
            acc[0] += p[:160]
            if opening:
                marks[...] += p[160:]
            p = jnp.dot(
                jnp.concatenate(lows, axis=1), cell_hots8[slots, :], preferred_element_type=f32
            )
            acc[1] += p * (m * (1.0 / LIFT))
            return c

        def interleave(even, odd):
            pair = jnp.concatenate([even, odd], axis=1).astype(bf16)
            return jnp.dot(pair, spread[...], preferred_element_type=f32)

        def place(half):
            acc[...] = jnp.zeros_like(acc)
            if opening:
                marks[...] = jnp.zeros_like(marks)
            lax.fori_loop(0, groups, functools.partial(scatter_group, half=half), 0)
            placed = interleave(acc[0, :80, :], acc[0, 80:, :]) + interleave(acc[1, :80, :], acc[1, 80:, :])
            pieces = ((0, 8), (8, 16)) if half else ((0, 0), (8, 24))
            if opening:
                mark = interleave(marks[:16, :], marks[16:, :])
            for n, j in pieces:
                if opening:
                    frozen[8 + j : 16 + j, :] = mark[n : n + 8]
                fixed = frozen[8 + j : 16 + j, :] > 0.5
                for v in range(V):
                    at = TOP + j
                    u[0, v, at : at + 8, :] = jnp.where(
                        fixed, placed[16 * v + n : 16 * v + n + 8], u[0, v, at : at + 8, :]
                    )

        place(0)

        for v in range(V):
            down_out[4 * v : 4 * v + 4, :] = u[0, v, TOP : TOP + 4, :]
            up_out[6 * v : 6 * v + 6, :] = u[0, v, TOP + NJ - 6 : TOP + NJ, :]
        if opening:
            down_out[20:22, :] = frozen[8:10, :]
            up_out[30:33, :] = frozen[5 + NJ : 8 + NJ, :]
        down, up = edges(it, 40 if opening else 32)

        @pl.when(has_low)
        def _():
            down.start()

        @pl.when(has_high)
        def _():
            up.start()

        place(1)

        pltpu.make_async_copy(send, send, send_sem).wait()

        def apply(rows, ts, v):
            return sum(inverse[v, w, rows, :] * ts[w] for w in range(V))

        def near_k(h, v, rows, at):
            x = u[h, v, at : at + 8, :]
            return (
                source[v, rows, :]
                + coupling[2, rows, :] * shift_k(x, -1)
                + coupling[3, rows, :] * shift_k(x, 1)
            )

        def near_rest(h, rows, at, along_k):
            ts = [
                along_k[v]
                + coupling[0, rows, :] * u[h, v, at - 1 : at + 7, :]
                + coupling[1, rows, :] * u[h, v, at + 1 : at + 9, :]
                for v in range(V)
            ]
            parity = (
                lax.broadcasted_iota(i32, (8, NK), 0) + lax.broadcasted_iota(i32, (8, NK), 1)
            ) & 1
            update = (frozen[rows, :] < 0.5) & (parity == h)
            for v in range(V):
                u[1 - h, v, at : at + 8, :] = jnp.where(
                    update, apply(rows, ts, v), u[h, v, at : at + 8, :]
                )

        def off_k(h, v, rows, at):
            x = u[h, v, at : at + 8, :]
            along = sum(a * shift_k(x, o) for o, a in zip(upwind_offsets, upwind_weights))
            return source[v, rows, :] - coupling[1, rows, :] * along

        def off_rest(h, rows, at, along_k):
            ts = []
            for v in range(V):
                along = sum(
                    a * u[h, v, at + o : at + o + 8, :]
                    for o, a in zip(upwind_offsets, upwind_weights)
                )
                ts.append(along_k[v] - coupling[0, rows, :] * along)
            update = frozen[rows, :] < 0.5
            for v in range(V):
                old = u[h, v, at : at + 8, :]
                u[1 - h, v, at : at + 8, :] = jnp.where(update, old + apply(rows, ts, v), old)

        def tile(t):
            return slice(8 * t + 8, 8 * t + 16), TOP + 8 * t

        def before(of_k, rest):
            for t in range(4):
                rows, at = tile(t)
                along_k = [of_k(0, v, rows, at) for v in range(V)]
                if t in (1, 2):
                    rest(0, rows, at, along_k)
                else:
                    for v in range(V):
                        part[v, 8 * t : 8 * t + 8, :] = along_k[v]

        def after(of_k, rest):
            for t in (0, 3):
                rows, at = tile(t)
                rest(0, rows, at, [part[v, 8 * t : 8 * t + 8, :] for v in range(V)])
            for t in (-1, 4):
                rows, at = tile(t)
                rest(0, rows, at, [of_k(0, v, rows, at) for v in range(V)])
            for t in range(4):
                rows, at = tile(t)
                rest(1, rows, at, [of_k(1, v, rows, at) for v in range(V)])

        @pl.when(is_near)
        def _():
            before(near_k, near_rest)

        @pl.when(jnp.logical_not(is_near))
        def _():
            before(off_k, off_rest)

        @pl.when(has_low)
        def _():
            up.wait_recv()
            for v in range(V):
                u[0, v, TOP - 6 : TOP, :] = up_in[it, 6 * v : 6 * v + 6, :]
            if opening:
                frozen[5:8, :] = up_in[it, 30:33, :]
                const_up.wait_recv()
                for n, (ref, at) in enumerate(constants):
                    ref[at + (slice(5, 8), slice(None))] = const_up_in[3 * n : 3 * n + 3, :]

        @pl.when(has_high)
        def _():
            down.wait_recv()
            for v in range(V):
                u[0, v, TOP + NJ : TOP + NJ + 4, :] = down_in[it, 4 * v : 4 * v + 4, :]
            if opening:
                frozen[8 + NJ : 10 + NJ, :] = down_in[it, 20:22, :]
                const_down.wait_recv()
                for n, (ref, at) in enumerate(constants):
                    ref[at + (slice(8 + NJ, 10 + NJ), slice(None))] = const_down_in[2 * n : 2 * n + 2, :]

        @pl.when(is_near)
        def _():
            after(near_k, near_rest)

        @pl.when(jnp.logical_not(is_near))
        def _():
            after(off_k, off_rest)

        @pl.when(has_low)
        def _():
            down.wait_send()
            if opening:
                const_down.wait_send()

        @pl.when(has_high)
        def _():
            up.wait_send()
            if opening:
                const_up.wait_send()

    sweep(0, True)

    def later(it, c):
        sweep(it, False)
        return c

    lax.fori_loop(1, ITERS, later, 0)

    for v in range(V):
        out[v] = u[0, v, TOP : TOP + NJ, :]


def on_device(field, source, block_inverse, coupling, donor_base, donor_weight, receiver_cell):
    blocks = donor_base.shape[2]
    hbm = pl.BlockSpec(memory_space=pl.ANY)
    result = pl.pallas_call(
        functools.partial(kernel, blocks),
        out_shape=jax.ShapeDtypeStruct((V, NJ, NK), f32),
        in_specs=[hbm] * 7,
        out_specs=pl.BlockSpec(memory_space=pltpu.VMEM),
        scratch_shapes=[
            pltpu.VMEM((V, NJ + 16, NK), f32),
            pltpu.VMEM((V, V, NJ + 16, NK), f32),
            pltpu.VMEM((4, NJ + 16, NK), f32),
            pltpu.VMEM((blocks, S), i32),
            pltpu.VMEM((4, blocks, S), f32),
            pltpu.VMEM((blocks, S), i32),
            pltpu.VMEM((2, V, 2 * TOP + NJ, NK), f32),
            pltpu.VMEM((480, NK // 2), bf16),
            pltpu.VMEM((480, NK // 2), f8),
            pltpu.VMEM((NK, NK), bf16),
            pltpu.VMEM((NK, NK), bf16),
            pltpu.VMEM((blocks, NK // 2, S), bf16),
            pltpu.VMEM((blocks, NK // 2, S), f8),
            pltpu.VMEM((blocks, 3, NJ, S), f32),
            pltpu.VMEM((blocks * S, NK // 2), bf16),
            pltpu.VMEM((blocks * S, NK // 2), f8),
            pltpu.VMEM((blocks, 8, S), f32),
            pltpu.VMEM((ITERS, blocks, 8, S), f32),
            pltpu.VMEM((2, 160, NK // 2), f32),
            pltpu.VMEM((32, NK // 2), f32),
            pltpu.VMEM((NJ + 16, NK), f32),
            pltpu.VMEM((V, NJ, NK), f32),
            pltpu.VMEM((24, NK), f32),
            pltpu.VMEM((40, NK), f32),
            pltpu.VMEM((ITERS, 24, NK), f32),
            pltpu.VMEM((ITERS, 40, NK), f32),
            pltpu.VMEM((72, NK), f32),
            pltpu.VMEM((104, NK), f32),
            pltpu.VMEM((72, NK), f32),
            pltpu.VMEM((104, NK), f32),
            pltpu.SemaphoreType.DMA,
            pltpu.SemaphoreType.DMA((ITERS, blocks // G)),
            pltpu.SemaphoreType.DMA((4,)),
            pltpu.SemaphoreType.DMA((ITERS, 4)),
            pltpu.SemaphoreType.DMA((7,)),
        ],
        compiler_params=pltpu.CompilerParams(
            collective_id=0, has_side_effects=True, vmem_limit_bytes=63 * 2**20
        ),
    )(
        field[0, 0],
        source[0, 0],
        block_inverse[0, 0],
        coupling[0, 0],
        donor_base[0, 0],
        donor_weight[0, 0],
        receiver_cell[0, 0],
    )
    return result[None, None]


def solution(mesh):
    in_specs = (
        P("group", "blk", None, None, None),
        P("group", "blk", None, None, None),
        P("group", "blk", None, None, None, None),
        P("group", "blk", None, None, None),
        P("group", "blk", None, None),
        P("group", "blk", None, None, None),
        P("group", "blk", None, None),
    )
    out_specs = P("group", "blk", None, None, None)
    return jax.shard_map(
        on_device, mesh=mesh, in_specs=in_specs, out_specs=out_specs, check_vma=False
    )
```

```python
import functools

import jax
import jax.numpy as jnp
from jax import lax
from jax.experimental import pallas as pl
from jax.experimental.pallas import tpu as pltpu
from jax.sharding import PartitionSpec as P

ITERS = 4
V = 5
NJ = 32
NK = 512
S = 256
TOP = 16
G = 8

upwind_offsets = (-3, -2, -1, 0, 1, 2)
upwind_weights = (-2.0 / 60.0, 15.0 / 60.0, -60.0 / 60.0, 20.0 / 60.0, 30.0 / 60.0, -3.0 / 60.0)

f32, bf16, i32 = jnp.float32, jnp.bfloat16, jnp.int32
f8 = jnp.float8_e4m3fn
LIFT = 65536.0
MESH = pl.DeviceIdType.MESH


def shift_k(x, o):
    if o == 0:
        return x
    n = x.shape[1]
    col = lax.broadcasted_iota(i32, x.shape, 1)
    rolled = pltpu.roll(x, (-o) % n, axis=1)
    keep = (col + o >= 0) & (col + o < n)
    return jnp.where(keep, rolled, 0.0)


def split(x):
    hi = x.astype(bf16)
    return hi, (x - hi.astype(f32)).astype(bf16)


def largest(x):
    m = jnp.max(jnp.max(jnp.abs(x), axis=1, keepdims=True), axis=0, keepdims=True)
    return jnp.maximum(m, 1e-30)


def swap_columns(inverse):
    a = lax.broadcasted_iota(i32, (NK, NK), 1 if inverse else 0)
    c = lax.broadcasted_iota(i32, (NK, NK), 0 if inverse else 1)
    return jnp.where(a == 2 * (c & (NK // 2 - 1)) + (c >> 8), 1.0, 0.0).astype(bf16)


def make_table(u, tab, tab8, pick):
    a = jnp.concatenate([u[0, v, TOP : TOP + NJ, :] for v in range(V)], axis=0)
    m = largest(a)
    t = jnp.dot(
        jnp.concatenate(split(a * (LIFT / m)), axis=0), pick[...], preferred_element_type=f32
    )
    t0, t1 = t[:, : NK // 2], t[:, NK // 2 :]
    first = jnp.concatenate([t0[1:, :1], jnp.zeros((1, 1), f32)], axis=0)
    t2 = jnp.concatenate([t0[:, 1:], first], axis=1)
    for o, p in enumerate((t0, t1, t2)):
        tab[pl.ds(160 * o, 160), :] = p[:160].astype(bf16)
        tab8[pl.ds(160 * o, 160), :] = p[160:].astype(f8)
    return m * (1.0 / LIFT)


def one_hot(base):
    k = (base & (NK - 1)) >> 1
    return jnp.where(lax.broadcasted_iota(i32, (NK // 2, S), 0) == k, 1.0, 0.0)


def patterns(base, w):
    even = (base & 1) == 0
    row = lax.broadcasted_iota(i32, (NJ, S), 0)
    here, below = row == (base >> 9), row == (base >> 9) + 1
    zero = jnp.zeros_like(w[0])

    def spread(x, y):
        return jnp.where(here, x, jnp.where(below, y, 0.0))

    return (
        spread(jnp.where(even, w[0], zero), jnp.where(even, w[2], zero)),
        spread(jnp.where(even, w[1], w[0]), jnp.where(even, w[3], w[2])),
        spread(jnp.where(even, zero, w[1]), jnp.where(even, zero, w[3])),
    )


def interpolate(tab, tab8, hot, hot8, ps, undo):
    high = jnp.dot(tab[...], hot, preferred_element_type=f32)
    low = jnp.dot(tab8[...], hot8, preferred_element_type=f32)
    rows = []
    for v in range(V):
        total = None
        for o in range(3):
            at = 160 * o + 32 * v
            term = (high[at : at + 32] + low[at : at + 32]) * ps[o]
            total = term if total is None else total + term
        rows.append(jnp.sum(total, axis=0, keepdims=True))
    return jnp.concatenate(rows + [jnp.zeros((3, S), f32)], axis=0) * undo


def rows_of(half):
    r = lax.broadcasted_iota(i32, (16, S), 0)
    return r + 8 if half else jnp.where(r < 8, r, r + 16)


def kernel(
    blocks,
    field_hbm, source_hbm, inverse_hbm, coupling_hbm, base_hbm, weight_hbm, cell_hbm,
    out,
    source, inverse, coupling, base, weight, cell,
    u, tab, tab8, pick, spread, hots, hots8, pats, cell_hots, cell_hots8,
    send, recv, acc, marks, frozen, part,
    down_out, up_out, down_in, up_in, const_down_out, const_up_out, const_down_in, const_up_in,
    send_sem, recv_sem, hsend_sem, hrecv_sem, in_sem,
):
    g = lax.axis_index("group")
    b = lax.axis_index("blk")
    groups = blocks // G
    mine, within = b // G, b % G
    other = 1 - g
    is_near = g == 0
    has_low, has_high = b > 0, b < blocks - 1

    def block_rows(ref):
        return ref.at[0, :, pl.ds(TOP, NJ), :]

    loads = [
        pltpu.make_async_copy(a, c, in_sem.at[n])
        for n, (a, c) in enumerate(
            (
                (field_hbm, block_rows(u)),
                (base_hbm, base),
                (weight_hbm, weight),
                (cell_hbm, cell),
                (source_hbm, source.at[:, pl.ds(8, NJ), :]),
                (coupling_hbm, coupling.at[:, pl.ds(8, NJ), :]),
                (inverse_hbm, inverse.at[:, :, pl.ds(8, NJ), :]),
            )
        )
    ]
    for load in loads:
        load.start()

    barrier = pltpu.get_barrier_semaphore()

    def greet(d, c):
        pl.semaphore_signal(barrier, inc=1, device_id=(other, d), device_id_type=MESH)
        return c

    lax.fori_loop(0, blocks, greet, 0)

    for d in ((b + blocks - 1) % blocks, (b + 1) % blocks):
        pl.semaphore_signal(barrier, inc=1, device_id=(g, d), device_id_type=MESH)

    edge_tiles = (slice(0, 8), slice(8 + NJ, 16 + NJ))
    for v in range(V):
        u[0, v, 0:TOP, :] = jnp.zeros((TOP, NK), f32)
        u[0, v, TOP + NJ : 2 * TOP + NJ, :] = jnp.zeros((TOP, NK), f32)
    constants = (
        [(source, (v,)) for v in range(V)]
        + [(inverse, (v, w)) for v in range(V) for w in range(V)]
        + [(coupling, (n,)) for n in range(4)]
    )
    for ref, at in constants + [(frozen, ())]:
        for rows in edge_tiles:
            ref[at + (rows, slice(None))] = jnp.zeros((8, NK), f32)
    for ref in (down_out, up_out, const_down_out, const_up_out):
        ref[...] = jnp.zeros_like(ref)

    pick[...] = swap_columns(False)
    spread[...] = swap_columns(True)

    for load in loads[:3]:
        load.wait()

    def far_first(turn):
        return groups // 2 + ((turn + 1) // 2) * (1 - 2 * (turn % 2))

    def message(it, i, d):
        return pltpu.make_async_remote_copy(
            src_ref=send.at[d],
            dst_ref=recv.at[it, b],
            send_sem=send_sem,
            recv_sem=recv_sem.at[it, i],
            device_id=(other, d),
            device_id_type=MESH,
        )

    def ship(src, dst, n, direction, slot):
        return pltpu.make_async_remote_copy(
            src_ref=src,
            dst_ref=dst,
            send_sem=hsend_sem.at[n],
            recv_sem=hrecv_sem.at[slot, n],
            device_id=(g, b + direction),
            device_id_type=MESH,
        )

    def edges(it, rows):
        return (
            ship(down_out, down_in.at[it], 0, -1, it),
            ship(up_out.at[pl.ds(0, rows)], up_in.at[it, pl.ds(0, rows)], 1, 1, it),
        )

    def const_edges():
        return (
            ship(const_down_out, const_down_in, 2, -1, 0),
            ship(const_up_out, const_up_in, 3, 1, 0),
        )

    def sweep(it, opening):
        undo = make_table(u, tab, tab8, pick)

        def gather_group(turn):
            i = far_first(turn)
            dg = (mine + i) % groups
            first = pl.multiple_of(dg * G, G)
            if opening:
                bases = base[pl.ds(first, G), :]
                ws = [weight[q, pl.ds(first, G), :] for q in range(4)]
            for q in range(G):
                if opening:
                    hot = one_hot(bases[q : q + 1])
                    hot, hot8 = hot.astype(bf16), hot.astype(f8)
                    ps = patterns(bases[q : q + 1], [w[q : q + 1] for w in ws])
                    hots[first + q] = hot
                    hots8[first + q] = hot8
                    for o in range(3):
                        pats[first + q, o] = ps[o]
                else:
                    hot, hot8 = hots[first + q], hots8[first + q]
                    ps = [pats[first + q, o] for o in range(3)]
                send[first + q] = interpolate(tab, tab8, hot, hot8, ps, undo)
            return i, first

        def gather_two(n, c):
            sent = [gather_group(2 * n), gather_group(2 * n + 1)]
            if opening:

                @pl.when(n == 0)
                def _():
                    pl.semaphore_wait(barrier, blocks + 2)

            for i, first in sent:
                for q in range(G):
                    message(it, i, first + (within + q) % G).start()
            return c

        lax.fori_loop(0, groups // 2, gather_two, 0)

        if opening:
            for load in loads[3:]:
                load.wait()
            for n, (ref, at) in enumerate(constants):
                const_down_out[2 * n : 2 * n + 2, :] = ref[at + (slice(8, 10), slice(None))]
                const_up_out[3 * n : 3 * n + 3, :] = ref[at + (slice(5 + NJ, 8 + NJ), slice(None))]
            const_down, const_up = const_edges()

            @pl.when(has_low)
            def _():
                const_down.start()

            @pl.when(has_high)
            def _():
                const_up.start()


        def scatter_group(turn, c, half):
            i = far_first(turn)
            sg = (mine + groups - i) % groups
            first = pl.multiple_of(sg * G, G)
            if not half:
                pltpu.make_async_copy(
                    recv.at[it, pl.ds(first, G)], recv.at[it, pl.ds(first, G)], recv_sem.at[it, i]
                ).wait()
            cells = cell[pl.ds(first, G), :]
            slots = pl.ds(pl.multiple_of(first * S, S), G * S)
            if opening and not half:
                down_cells = jnp.transpose(cells.astype(f32)).astype(i32)
                for q in range(G):
                    hot = jnp.where(
                        lax.broadcasted_iota(i32, (S, NK // 2), 1)
                        == (down_cells[:, q : q + 1] & (NK - 1)) >> 1,
                        1.0,
                        0.0,
                    )
                    at = pl.ds(pl.multiple_of((first + q) * S, S), S)
                    cell_hots[at, :] = hot.astype(bf16)
                    cell_hots8[at, :] = hot.astype(f8)
            vals = [recv[it, first + q] for q in range(G)]
            m = largest(functools.reduce(jnp.maximum, [jnp.abs(x) for x in vals]))
            scale = LIFT / m
            highs, lows = [], []
            for q in range(G):
                r = cells[q : q + 1]
                hit = rows_of(half) == (r >> 9)
                even = (r & 1) == 0
                hits = (hit & even, hit & jnp.logical_not(even))
                high = vals[q].astype(bf16).astype(f32)
                low = (vals[q] - high) * scale
                rows = [jnp.where(x, high[v : v + 1], 0.0) for x in hits for v in range(V)]
                if opening:
                    rows += [jnp.where(x, 1.0, 0.0) for x in hits]
                highs.append(jnp.concatenate(rows, axis=0).astype(bf16))
                rows = [jnp.where(x, low[v : v + 1], 0.0) for x in hits for v in range(V)]
                lows.append(jnp.concatenate(rows, axis=0).astype(f8))
            p = jnp.dot(
                jnp.concatenate(highs, axis=1), cell_hots[slots, :], preferred_element_type=f32
            )
            acc[0] += p[:160]
            if opening:
                marks[...] += p[160:]
            p = jnp.dot(
                jnp.concatenate(lows, axis=1), cell_hots8[slots, :], preferred_element_type=f32
            )
            acc[1] += p * (m * (1.0 / LIFT))
            return c

        def interleave(even, odd):
            pair = jnp.concatenate([even, odd], axis=1).astype(bf16)
            return jnp.dot(pair, spread[...], preferred_element_type=f32)

        def place(half):
            acc[...] = jnp.zeros_like(acc)
            if opening:
                marks[...] = jnp.zeros_like(marks)
            if half:

                def two_groups(n, c):
                    scatter_group(2 * n, c, 1)
                    scatter_group(2 * n + 1, c, 1)
                    return c

                lax.fori_loop(0, groups // 2, two_groups, 0)
            else:
                lax.fori_loop(0, groups, functools.partial(scatter_group, half=0), 0)
            placed = interleave(acc[0, :80, :], acc[0, 80:, :]) + interleave(acc[1, :80, :], acc[1, 80:, :])
            pieces = ((0, 8), (8, 16)) if half else ((0, 0), (8, 24))
            if opening:
                mark = interleave(marks[:16, :], marks[16:, :])
            for n, j in pieces:
                if opening:
                    frozen[8 + j : 16 + j, :] = mark[n : n + 8]
                fixed = frozen[8 + j : 16 + j, :] > 0.5
                for v in range(V):
                    at = TOP + j
                    u[0, v, at : at + 8, :] = jnp.where(
                        fixed, placed[16 * v + n : 16 * v + n + 8], u[0, v, at : at + 8, :]
                    )

        place(0)

        for v in range(V):
            down_out[4 * v : 4 * v + 4, :] = u[0, v, TOP : TOP + 4, :]
            up_out[6 * v : 6 * v + 6, :] = u[0, v, TOP + NJ - 6 : TOP + NJ, :]
        if opening:
            down_out[20:22, :] = frozen[8:10, :]
            up_out[30:33, :] = frozen[5 + NJ : 8 + NJ, :]
        down, up = edges(it, 40 if opening else 32)

        @pl.when(has_low)
        def _():
            down.start()

        @pl.when(has_high)
        def _():
            up.start()

        place(1)

        pltpu.make_async_copy(send, send, send_sem).wait()

        def apply(rows, ts, v):
            return sum(inverse[v, w, rows, :] * ts[w] for w in range(V))

        def near_k(h, v, rows, at):
            x = u[h, v, at : at + 8, :]
            return (
                source[v, rows, :]
                + coupling[2, rows, :] * shift_k(x, -1)
                + coupling[3, rows, :] * shift_k(x, 1)
            )

        def near_rest(h, rows, at, along_k):
            ts = [
                along_k[v]
                + coupling[0, rows, :] * u[h, v, at - 1 : at + 7, :]
                + coupling[1, rows, :] * u[h, v, at + 1 : at + 9, :]
                for v in range(V)
            ]
            parity = (
                lax.broadcasted_iota(i32, (8, NK), 0) + lax.broadcasted_iota(i32, (8, NK), 1)
            ) & 1
            update = (frozen[rows, :] < 0.5) & (parity == h)
            for v in range(V):
                u[1 - h, v, at : at + 8, :] = jnp.where(
                    update, apply(rows, ts, v), u[h, v, at : at + 8, :]
                )

        def off_k(h, v, rows, at):
            x = u[h, v, at : at + 8, :]
            along = sum(a * shift_k(x, o) for o, a in zip(upwind_offsets, upwind_weights))
            return source[v, rows, :] - coupling[1, rows, :] * along

        def off_rest(h, rows, at, along_k):
            ts = []
            for v in range(V):
                along = sum(
                    a * u[h, v, at + o : at + o + 8, :]
                    for o, a in zip(upwind_offsets, upwind_weights)
                )
                ts.append(along_k[v] - coupling[0, rows, :] * along)
            update = frozen[rows, :] < 0.5
            for v in range(V):
                old = u[h, v, at : at + 8, :]
                u[1 - h, v, at : at + 8, :] = jnp.where(update, old + apply(rows, ts, v), old)

        def tile(t):
            return slice(8 * t + 8, 8 * t + 16), TOP + 8 * t

        def before(of_k, rest):
            for t in range(4):
                rows, at = tile(t)
                along_k = [of_k(0, v, rows, at) for v in range(V)]
                if t in (1, 2):
                    rest(0, rows, at, along_k)
                else:
                    for v in range(V):
                        part[v, 8 * t : 8 * t + 8, :] = along_k[v]

        def after(of_k, rest):
            for t in (0, 3):
                rows, at = tile(t)
                rest(0, rows, at, [part[v, 8 * t : 8 * t + 8, :] for v in range(V)])
            for t in (-1, 4):
                rows, at = tile(t)
                rest(0, rows, at, [of_k(0, v, rows, at) for v in range(V)])
            for t in range(4):
                rows, at = tile(t)
                rest(1, rows, at, [of_k(1, v, rows, at) for v in range(V)])

        @pl.when(is_near)
        def _():
            before(near_k, near_rest)

        @pl.when(jnp.logical_not(is_near))
        def _():
            before(off_k, off_rest)

        @pl.when(has_low)
        def _():
            up.wait_recv()
            for v in range(V):
                u[0, v, TOP - 6 : TOP, :] = up_in[it, 6 * v : 6 * v + 6, :]
            if opening:
                frozen[5:8, :] = up_in[it, 30:33, :]
                const_up.wait_recv()
                for n, (ref, at) in enumerate(constants):
                    ref[at + (slice(5, 8), slice(None))] = const_up_in[3 * n : 3 * n + 3, :]

        @pl.when(has_high)
        def _():
            down.wait_recv()
            for v in range(V):
                u[0, v, TOP + NJ : TOP + NJ + 4, :] = down_in[it, 4 * v : 4 * v + 4, :]
            if opening:
                frozen[8 + NJ : 10 + NJ, :] = down_in[it, 20:22, :]
                const_down.wait_recv()
                for n, (ref, at) in enumerate(constants):
                    ref[at + (slice(8 + NJ, 10 + NJ), slice(None))] = const_down_in[2 * n : 2 * n + 2, :]

        @pl.when(is_near)
        def _():
            after(near_k, near_rest)

        @pl.when(jnp.logical_not(is_near))
        def _():
            after(off_k, off_rest)

        @pl.when(has_low)
        def _():
            down.wait_send()
            if opening:
                const_down.wait_send()

        @pl.when(has_high)
        def _():
            up.wait_send()
            if opening:
                const_up.wait_send()

    sweep(0, True)

    def later(it, c):
        sweep(it, False)
        return c

    lax.fori_loop(1, ITERS, later, 0)

    for v in range(V):
        out[v] = u[0, v, TOP : TOP + NJ, :]


def on_device(field, source, block_inverse, coupling, donor_base, donor_weight, receiver_cell):
    blocks = donor_base.shape[2]
    hbm = pl.BlockSpec(memory_space=pl.ANY)
    result = pl.pallas_call(
        functools.partial(kernel, blocks),
        out_shape=jax.ShapeDtypeStruct((V, NJ, NK), f32),
        in_specs=[hbm] * 7,
        out_specs=pl.BlockSpec(memory_space=pltpu.VMEM),
        scratch_shapes=[
            pltpu.VMEM((V, NJ + 16, NK), f32),
            pltpu.VMEM((V, V, NJ + 16, NK), f32),
            pltpu.VMEM((4, NJ + 16, NK), f32),
            pltpu.VMEM((blocks, S), i32),
            pltpu.VMEM((4, blocks, S), f32),
            pltpu.VMEM((blocks, S), i32),
            pltpu.VMEM((2, V, 2 * TOP + NJ, NK), f32),
            pltpu.VMEM((480, NK // 2), bf16),
            pltpu.VMEM((480, NK // 2), f8),
            pltpu.VMEM((NK, NK), bf16),
            pltpu.VMEM((NK, NK), bf16),
            pltpu.VMEM((blocks, NK // 2, S), bf16),
            pltpu.VMEM((blocks, NK // 2, S), f8),
            pltpu.VMEM((blocks, 3, NJ, S), f32),
            pltpu.VMEM((blocks * S, NK // 2), bf16),
            pltpu.VMEM((blocks * S, NK // 2), f8),
            pltpu.VMEM((blocks, 8, S), f32),
            pltpu.VMEM((ITERS, blocks, 8, S), f32),
            pltpu.VMEM((2, 160, NK // 2), f32),
            pltpu.VMEM((32, NK // 2), f32),
            pltpu.VMEM((NJ + 16, NK), f32),
            pltpu.VMEM((V, NJ, NK), f32),
            pltpu.VMEM((24, NK), f32),
            pltpu.VMEM((40, NK), f32),
            pltpu.VMEM((ITERS, 24, NK), f32),
            pltpu.VMEM((ITERS, 40, NK), f32),
            pltpu.VMEM((72, NK), f32),
            pltpu.VMEM((104, NK), f32),
            pltpu.VMEM((72, NK), f32),
            pltpu.VMEM((104, NK), f32),
            pltpu.SemaphoreType.DMA,
            pltpu.SemaphoreType.DMA((ITERS, blocks // G)),
            pltpu.SemaphoreType.DMA((4,)),
            pltpu.SemaphoreType.DMA((ITERS, 4)),
            pltpu.SemaphoreType.DMA((7,)),
        ],
        compiler_params=pltpu.CompilerParams(
            collective_id=0, has_side_effects=True, vmem_limit_bytes=63 * 2**20
        ),
    )(
        field[0, 0],
        source[0, 0],
        block_inverse[0, 0],
        coupling[0, 0],
        donor_base[0, 0],
        donor_weight[0, 0],
        receiver_cell[0, 0],
    )
    return result[None, None]


def solution(mesh):
    in_specs = (
        P("group", "blk", None, None, None),
        P("group", "blk", None, None, None),
        P("group", "blk", None, None, None, None),
        P("group", "blk", None, None, None),
        P("group", "blk", None, None),
        P("group", "blk", None, None, None),
        P("group", "blk", None, None),
    )
    out_specs = P("group", "blk", None, None, None)
    return jax.shard_map(
        on_device, mesh=mesh, in_specs=in_specs, out_specs=out_specs, check_vma=False
    )
```
